128 devices in a mesh: dp: 2 (over x_lo), expert: 32 (over y, z, core), tensor: 2 (over x_hi).
Axes of the slice: x: 4 (x_hi: 2, x_lo: 2; x = x_hi * 2 + x_lo), y: 4, z: 4, core: 2. Of those that a mesh axis runs over, the one named last changes fastest.
Arguments:
- hidden_in: bfloat16 [8192, 2048], P(('dp', 'expert')), may hold values from -6 to 6
- prenorm: bfloat16 [2048], P(('dp', 'expert')), may hold values from 0.5 to 1.5
- query_proj: bfloat16 [2048, 3072], P(('dp', 'expert'), 'tensor'), may hold values from -0.125 to 0.125
- latent_proj: bfloat16 [2048, 576], P(('dp', 'expert')), may hold values from -0.125 to 0.125
- midnorm: bfloat16 [512], P(('dp', 'expert')), may hold values from 0.5 to 1.5
- expand_proj: bfloat16 [512, 4096], P(('dp', 'expert'), 'tensor'), may hold values from -0.25 to 0.25
- output_proj: bfloat16 [2048, 2048], P('tensor', ('dp', 'expert')), may hold values from -0.5 to 0.5
- postnorm: bfloat16 [2048], P(('dp', 'expert')), may hold values from 0.5 to 1.5
- shared_gate: bfloat16 [2048, 2816], P(('dp', 'expert'), 'tensor'), may hold values from -0.125 to 0.125
- shared_up: bfloat16 [2048, 2816], P(('dp', 'expert'), 'tensor'), may hold values from -0.125 to 0.125
- shared_down: bfloat16 [2816, 2048], P('tensor', ('dp', 'expert')), may hold values from -0.109375 to 0.109375
- expert_gate: bfloat16 [32, 2048, 1408], P('expert', None, 'tensor'), may hold values from -0.125 to 0.125
- expert_up: bfloat16 [32, 2048, 1408], P('expert', None, 'tensor'), may hold values from -0.125 to 0.125
- expert_down: bfloat16 [32, 1408, 2048], P('expert', 'tensor'), may hold values from -0.15625 to 0.15625
- segments: int32 [8192], replicated, may hold values from 0 to 7, as said below
- routes: int32 [8192, 6], P(('dp', 'expert')), may hold values from 0 to 31, all different within a row; in each aligned block of 128 rows (0 to 127, 128 to 255, ...) at most 30 rows name the same one
- route_weights: float32 [8192, 6], P(('dp', 'expert')), may hold values from 0.3 to 1
- cotangent: bfloat16 [8192, 2048], P(('dp', 'expert')), may hold values from -6 to 6
Outputs:
- block_out: bfloat16 [8192, 2048], P(('dp', 'expert'))
- input_grad: float32 [8192, 2048], P(('dp', 'expert'))
- prenorm_grad: float32 [2048], P(('dp', 'expert'))
- query_grad: float32 [2048, 3072], P(('dp', 'expert'), 'tensor')
- latent_grad: float32 [2048, 576], P(('dp', 'expert'))
- midnorm_grad: float32 [512], P(('dp', 'expert'))
- expand_grad: float32 [512, 4096], P(('dp', 'expert'), 'tensor')
- output_grad: float32 [2048, 2048], P('tensor', ('dp', 'expert'))
- postnorm_grad: float32 [2048], P(('dp', 'expert'))
- shared_gate_grad: float32 [2048, 2816], P(('dp', 'expert'), 'tensor')
- shared_up_grad: float32 [2048, 2816], P(('dp', 'expert'), 'tensor')
- shared_down_grad: float32 [2816, 2048], P('tensor', ('dp', 'expert'))
- expert_gate_grad: float32 [32, 2048, 1408], P('expert', None, 'tensor')
- expert_up_grad: float32 [32, 2048, 1408], P('expert', None, 'tensor')
- expert_down_grad: float32 [32, 1408, 2048], P('expert', 'tensor')
The draws below stay inside these ranges and needn't reach their ends.
Inputs may be any that keep to these rules, and one draw needn't show every extreme that they name: `segments`: ids never fall along the tokens; the r-th block of 4096 tokens starts with id 4 r and holds ids 4 r to 4 r + 3 only. `routes`: each token names 6 different experts; among the 128 tokens of one device (aligned blocks) no expert is named more than 30 times.
All inputs are finite; a program needn't handle non-finite values.
Results may differ from the reference program's by a relative error of at most 0.023.
Values may be sent and summed in bfloat16 or wider, within the bound.
No kernel may reach another device: no remote copies, remote signals or barrier semaphores. Data moves between devices by JAX's collectives and lax.ppermute only.
A program may use at most 256 MiB of HBM per device.

```python
import math
import jax
import jax.numpy as jnp
import numpy as np
from jax import lax

D = 2048
H = 16
QN = 128
QR = 64
DV = 128
LATENT = 512
F = 1408
TOPK = 6
WIN = 1024
DOCS = 4
TOK_DEV = 128
FS = 2816
EXPERTS = 32
CAP = 30
ROW_LEN = 4096
ROWS = 2
TOKENS = 8192
N_EXPERT = 32


def draw_segments(key, part):
    key = jax.random.fold_in(key, 7)
    cut_points = jnp.sort(jax.random.randint(key, (ROWS, DOCS - 1), 1, ROW_LEN), axis=1)
    positions = jnp.arange(ROW_LEN, dtype=jnp.int32)
    docs_before = jnp.sum((positions[None, :, None] >= cut_points[:, None, :]).astype(jnp.int32), axis=2)
    row_base = jnp.arange(ROWS, dtype=jnp.int32)[:, None] * DOCS
    return (row_base + docs_before).reshape(ROWS * ROW_LEN).astype(jnp.int32)


def levels(own_key, extent, split, least, largest):
    factor_of = 1.0
    for dim, parts in split:
        steps = jax.random.uniform(jax.random.fold_in(jax.random.fold_in(own_key, 6), dim), (parts,), jnp.float32, least / len(split), largest / len(split))
        factor_of = factor_of * jnp.repeat(jnp.exp(steps), extent[dim] // parts).reshape((-1,) + (1,) * (len(extent) - 1 - dim))
    return factor_of


def routed_block(own_key, own, number, rows, count, top, most, skew):
    order = jax.random.permutation(own_key, count)
    heavy_load, ordinary = portions_of(count, rows * top, most, skew, True), portions_of(count, rows * top, most, skew, False)
    places = jnp.arange(count)

    def named(lengths, turn):
        used = int((lengths > 0).sum())
        fixed = max(1, used // 4)
        shifted = fixed + (places - fixed + turn * (used - fixed)) % max(1, count - fixed)
        return jnp.zeros((count,), jnp.int32).at[order[jnp.where(places < fixed, places, shifted)]].set(jnp.asarray(lengths, jnp.int32))

    lengths = jnp.where(number % 4 == 0, named(heavy_load, number // 4), named(ordinary, number - number // 4 - 1))
    mixed = jax.random.permutation(jax.random.fold_in(own, 3), count)
    source_of, sink = mixed[0:count // 2 * 2:2], mixed[1:count // 2 * 2:2]
    room = jnp.minimum(lengths[source_of] - 1, most - lengths[sink]) // 2
    room = jnp.where((source_of == order[0]) | (sink == order[0]) | (lengths[sink] == 0), 0, jnp.maximum(room, 0))
    shifted = jax.random.randint(jax.random.fold_in(own, 4), (count // 2,), 0, 1 << 20) % (room + 1)
    lengths = lengths.at[source_of].add(-shifted).at[sink].add(shifted)
    items = jnp.searchsorted(jnp.cumsum(lengths), jnp.arange(rows * top), side="right").astype(jnp.int32)
    grid = items.reshape(top, rows).T
    grid = grid[jax.random.permutation(jax.random.fold_in(own, 1), rows)]
    turn = jax.random.randint(jax.random.fold_in(own, 2), (rows, 1), 0, top)
    return jnp.take_along_axis(grid, (jnp.arange(top)[None, :] + turn) % top, axis=1)


def portions_of(amount, total, limit, skew, full):
    weights = [(1 << 20) // math.isqrt(rank ** skew) + 1 for rank in range(1, amount + 1)]
    largest = limit if full else min(limit, max(-(-total // amount), total * weights[0] // sum(weights)))
    least = 1 if total - largest >= amount - 1 else 0
    counts, rest = [largest] + [least] * (amount - 1), total - largest - least * (amount - 1)
    while rest > 0:
        free = [i for i in range(1, amount) if counts[i] < largest] or [i for i in range(1, amount) if counts[i] < limit]
        mass, left = sum([weights[i] for i in free]), rest
        for i in free:
            more = min(limit - counts[i], max(1, left * weights[i] // mass), rest)
            counts[i] = counts[i] + more
            rest = rest - more
    return np.array(counts)


def scatter_about(key, dims, scale, reach, cuts=(), kind=jnp.bfloat16):
    loudness = levels(key, dims, cuts, -0.22, 0.18) if cuts else 1.0
    values = jax.random.normal(key, dims, jnp.float32) * scale * loudness
    return jnp.minimum(jnp.maximum(values, -reach), reach).astype(kind)


def setup_inputs(seed: int = 0) -> dict:
    key_list = jax.random.split(jax.random.key(seed), 19)
    hidden_in = scatter_about(key_list[0], (TOKENS, D), 1.0, 6.0, ((0, 64),))
    prenorm = jnp.clip(1.0 + 0.1 * jax.random.normal(key_list[1], (D,), jnp.float32), 0.5, 1.5).astype(jnp.bfloat16)
    query_proj = scatter_about(key_list[2], (D, H * (QN + QR)), D ** -0.5, 0.125, ((0, 64), (1, 2)))
    latent_proj = scatter_about(key_list[3], (D, LATENT + QR), D ** -0.5, 0.125, ((0, 64),))
    midnorm = jnp.clip(1.0 + 0.1 * jax.random.normal(key_list[4], (LATENT,), jnp.float32), 0.5, 1.5).astype(jnp.bfloat16)
    expand_proj = scatter_about(key_list[5], (LATENT, H * (QN + DV)), LATENT ** -0.5, 0.25, ((0, 64), (1, 2)))
    output_proj = scatter_about(key_list[6], (H * DV, D), (H * DV // 16) ** -0.5, 0.5, ((0, 2), (1, 64)))
    postnorm = jnp.clip(1.0 + 0.1 * jax.random.normal(key_list[7], (D,), jnp.float32), 0.5, 1.5).astype(jnp.bfloat16)
    shared_gate = scatter_about(key_list[8], (D, FS), D ** -0.5, 0.125, ((0, 64), (1, 2)))
    shared_up = scatter_about(key_list[9], (D, FS), D ** -0.5, 0.125, ((0, 64), (1, 2)))
    shared_down = scatter_about(key_list[10], (FS, D), FS ** -0.5, 0.109375, ((0, 2), (1, 64)))
    expert_gate = scatter_about(key_list[11], (EXPERTS, D, F), D ** -0.5, 0.125, ((0, 32), (2, 2)))
    expert_up = scatter_about(key_list[12], (EXPERTS, D, F), D ** -0.5, 0.125, ((0, 32), (2, 2)))
    expert_down = scatter_about(key_list[13], (EXPERTS, F, D), F ** -0.5, 0.15625, ((0, 32), (1, 2)))
    segments = draw_segments(jax.random.fold_in(key_list[18], 71), 0)
    routes_keys = jax.random.split(jax.random.fold_in(key_list[15], 1), TOKENS // TOK_DEV)
    routes_turns = jax.random.permutation(jax.random.fold_in(key_list[15], 3), TOKENS // TOK_DEV)
    routes = jax.vmap(lambda own, number: routed_block(jax.random.fold_in(key_list[15], 2), own, number, TOK_DEV, EXPERTS, TOPK, CAP, 2))(routes_keys, routes_turns).reshape((TOKENS, TOPK))
    route_weights = jnp.clip(0.3 + 0.7 * jax.random.uniform(key_list[16], (TOKENS, TOPK), jnp.float32) ** levels(key_list[16], (TOKENS, TOPK), ((0, 64),), -0.2, 0.2), 0.3, 1.0)
    cotangent = scatter_about(key_list[17], (TOKENS, D), 1.0, 6.0, ((0, 64),))
    return {"hidden_in": hidden_in, "prenorm": prenorm, "query_proj": query_proj, "latent_proj": latent_proj, "midnorm": midnorm, "expand_proj": expand_proj, "output_proj": output_proj, "postnorm": postnorm, "shared_gate": shared_gate, "shared_up": shared_up, "shared_down": shared_down, "expert_gate": expert_gate, "expert_up": expert_up, "expert_down": expert_down, "segments": segments, "routes": routes, "route_weights": route_weights, "cotangent": cotangent}


@jax.custom_vjp
def low(v):
    return lax.optimization_barrier(v.astype(jnp.bfloat16)).astype(jnp.float32)

@jax.custom_vjp
def low_back(v):
    return v

def low_keep(v):
    return (low(v), None)

def low_pass(kept, grad):
    return (grad,)

def back_keep(v):
    return (v, None)

def back_low(kept, grad):
    return (low(grad),)
low.defvjp(low_keep, low_pass)
low_back.defvjp(back_keep, back_low)
epsilon = 1e-06
neg_big = -1e+30
highest = lax.Precision.HIGHEST

def round_both(values):
    return low(low_back(values))

def matmul(left_op, right_op):
    return jnp.dot(left_op, right_op, precision=highest, preferred_element_type=jnp.float32)

def rms_norm(values, gain_vec):
    return values * lax.rsqrt(lax.optimization_barrier(jnp.mean(values * values, axis=-1, keepdims=True)) + epsilon) * gain_vec

def rope_tables(positions, width):
    half_width = width // 2
    frequency = jnp.exp(-math.log(10000.0) * jnp.arange(half_width, dtype=jnp.float32) * (2.0 / width))
    angles = positions[:, None] * frequency[None, :]
    return (jnp.cos(angles), jnp.sin(angles))

def rotate(values, cosine, sine_tab):
    half_width = values.shape[-1] // 2
    first_half = values[..., :half_width]
    second_half = values[..., half_width:]
    return jnp.concatenate([first_half * cosine - second_half * sine_tab, first_half * sine_tab + second_half * cosine], axis=-1)

def attend(q_full, latent, segments):
    tok_total = q_full.shape[0]
    block_rows = math.gcd(tok_total, 512)
    key_rows = WIN + block_rows
    score_scale = 1.0 / math.sqrt(QN + QR)
    latent_pad = jnp.concatenate([jnp.zeros((WIN, latent.shape[1]), jnp.float32), latent], axis=0)
    seg_pad = jnp.concatenate([jnp.full((WIN,), -1, jnp.int32), segments], axis=0)

    def one_block(block_index):
        row_start = block_index * block_rows
        queries = lax.dynamic_slice_in_dim(q_full, row_start, block_rows, 0)
        keys_here = lax.dynamic_slice_in_dim(latent_pad, row_start, key_rows, 0)
        seg_query = lax.dynamic_slice_in_dim(segments, row_start, block_rows, 0)
        seg_keys = lax.dynamic_slice_in_dim(seg_pad, row_start, key_rows, 0)
        offsets = jnp.arange(block_rows, dtype=jnp.int32)[:, None] + WIN - jnp.arange(key_rows, dtype=jnp.int32)[None, :]
        visible = (seg_query[:, None] == seg_keys[None, :]) & (offsets >= 0) & (offsets < WIN)
        raw = low_back(jnp.einsum('qhc,kc->hqk', queries, keys_here, precision=highest)) * score_scale
        logits = jnp.where(visible[None], raw, neg_big)
        row_max = lax.optimization_barrier(jnp.max(logits, axis=2, keepdims=True))
        expo_vals = jnp.exp(logits - row_max)
        attn_probs = low(expo_vals / lax.optimization_barrier(jnp.sum(expo_vals, axis=2, keepdims=True)))
        return low_back(jnp.einsum('hqk,kc->qhc', attn_probs, keys_here[:, :LATENT], precision=highest))
    blocks = lax.map(jax.checkpoint(one_block), jnp.arange(tok_total // block_rows, dtype=jnp.int32))
    return blocks.reshape(tok_total, q_full.shape[1], LATENT)

def experts_apply(h_two, expert_gate, expert_up, expert_down, routes, route_weights):
    tok_total = h_two.shape[0]
    entries = tok_total * TOPK
    flat_routes = routes.reshape(entries)
    flat_weights = jnp.concatenate([route_weights.reshape(entries), jnp.zeros((1,), jnp.float32)])
    padded_rows = jnp.concatenate([h_two, jnp.zeros((1, D), jnp.float32)], axis=0)
    most_rows = ROWS * N_EXPERT * CAP

    def one_expert(inputs_each):
        w_gate, w_up, w_down, ident = inputs_each
        picked = jnp.nonzero(flat_routes == ident, size=most_rows, fill_value=entries)[0].astype(jnp.int32)
        token_ids = picked // TOPK
        expert_rows = padded_rows[token_ids]
        gate_pre = low_back(matmul(expert_rows, w_gate))
        up_pre = low_back(matmul(expert_rows, w_up))
        hidden = low(gate_pre * jax.nn.sigmoid(gate_pre) * up_pre)
        result = round_both(matmul(hidden, w_down))
        return (result * flat_weights[picked][:, None], token_ids)
    contrib, token_ids = lax.map(jax.checkpoint(one_expert), (expert_gate, expert_up, expert_down, jnp.arange(EXPERTS, dtype=jnp.int32)))
    summed = jnp.zeros((tok_total + 1, D), jnp.float32).at[token_ids.reshape(-1)].add(contrib.reshape(-1, D))
    return summed[:tok_total]

def forward(hidden_in, prenorm, query_proj, latent_proj, midnorm, expand_proj, output_proj, postnorm, shared_gate, shared_up, shared_down, expert_gate, expert_up, expert_down, segments, routes, route_weights):
    tok_total = hidden_in.shape[0]
    positions = (jnp.arange(tok_total, dtype=jnp.int32) % ROW_LEN).astype(jnp.float32)
    cosine, sine_tab = rope_tables(positions, QR)
    h_one = low(rms_norm(hidden_in, prenorm))
    queries = low_back(matmul(h_one, query_proj)).reshape(tok_total, H, QN + QR)
    q_nope = low(queries[:, :, :QN])
    kv_pre = low_back(matmul(h_one, latent_proj))
    latent = low(jnp.concatenate([rms_norm(kv_pre[:, :LATENT], midnorm), rotate(kv_pre[:, LATENT:], cosine, sine_tab)], axis=1))
    w_heads = expand_proj.reshape(LATENT, H, QN + DV)
    q_latent = low_back(jnp.einsum('thn,chn->thc', q_nope, w_heads[:, :, :QN], precision=highest))
    q_rotated = rotate(queries[:, :, QN:], cosine[:, None, :], sine_tab[:, None, :])
    q_full = low(jnp.concatenate([q_latent, q_rotated], axis=2))
    o_latent = low(attend(q_full, latent, segments))
    o_heads = round_both(jnp.einsum('thc,chv->thv', o_latent, w_heads[:, :, QN:], precision=highest))
    mid = hidden_in + low_back(matmul(o_heads.reshape(tok_total, H * DV), output_proj))
    h_two = low(rms_norm(mid, postnorm))
    s_gate = low_back(matmul(h_two, shared_gate))
    s_up = low_back(matmul(h_two, shared_up))
    s_out = low_back(matmul(low(s_gate * jax.nn.sigmoid(s_gate) * s_up), shared_down))
    routed = experts_apply(h_two, expert_gate, expert_up, expert_down, routes, route_weights)
    return mid + s_out + routed

def reference(hidden_in, prenorm, query_proj, latent_proj, midnorm, expand_proj, output_proj, postnorm, shared_gate, shared_up, shared_down, expert_gate, expert_up, expert_down, segments, routes, route_weights, cotangent):
    params = tuple((array_in.astype(jnp.float32) for array_in in (hidden_in, prenorm, query_proj, latent_proj, midnorm, expand_proj, output_proj, postnorm, shared_gate, shared_up, shared_down, expert_gate, expert_up, expert_down)))
    weights_f = route_weights.astype(jnp.float32)

    def closed(*arrays):
        return forward(*arrays, segments, routes, weights_f)
    block_out, pull = jax.vjp(closed, *params)
    grads = pull(cotangent.astype(jnp.float32))
    return (block_out.astype(jnp.bfloat16), grads[0], grads[1], grads[2], grads[3], grads[4], grads[5], grads[6], grads[7], grads[8], grads[9], grads[10], grads[11], grads[12], grads[13])
```

```python
import math

import jax
import jax.numpy as jnp
from jax import lax
from jax.sharding import Mesh, PartitionSpec as P

D = 2048
QN = 128
QR = 64
DV = 128
LATENT = 512
TOPK = 6
WIN = 1024
SLOTS = 32

epsilon = 1e-06
neg_big = -1e30
f32 = jnp.float32
bf16 = jnp.bfloat16
PLANE = ("y", "z")
EXPERT = ("y", "z", "core")


def swapped(block, axis):
    return lax.ppermute(block, axis, [(0, 1), (1, 0)])


def chip_shift(block, distance):
    chips = range(16)
    route = [(i - distance, i) for i in chips if i - distance in chips]
    return lax.ppermute(block, PLANE, route)


def matmul(left_op, right_op):
    return jnp.dot(left_op, right_op, preferred_element_type=f32)


def matmul_tn(left_op, right_op):
    return lax.dot_general(
        left_op, right_op, (((0,), (0,)), ((), ())), preferred_element_type=f32
    )


def matmul_nt(left_op, right_op):
    return lax.dot_general(
        left_op, right_op, (((1,), (1,)), ((), ())), preferred_element_type=f32
    )


def pair_sum(part, axis):
    low = lax.optimization_barrier(part.astype(bf16))
    return low.astype(f32) + swapped(low, axis).astype(f32)


def split_low(values):
    high = values.astype(bf16)
    return high, (values - high.astype(f32)).astype(bf16)


def rms_forward(values, gain_vec):
    inverse = lax.rsqrt(jnp.mean(values * values, axis=-1, keepdims=True) + epsilon)
    return (values * inverse * gain_vec, inverse)


def rms_backward(values, inverse, gain_vec, upstream):
    scaled = upstream * gain_vec
    inner_mean = jnp.mean(scaled * values, axis=-1, keepdims=True)
    back_values = inverse * (scaled - values * inner_mean * inverse * inverse)
    gain_grad = jnp.sum(upstream * values * inverse, axis=0)
    return (back_values, gain_grad)


def rope_tables(positions, width):
    half_width = width // 2
    frequency = jnp.exp(
        -math.log(10000.0) * jnp.arange(half_width, dtype=f32) * (2.0 / width)
    )
    angles = positions[:, None] * frequency[None, :]
    return (jnp.cos(angles), jnp.sin(angles))


def rotate(values, cosine, sine_tab):
    half_width = values.shape[-1] // 2
    first_half = values[..., :half_width]
    second_half = values[..., half_width:]
    return jnp.concatenate(
        [
            first_half * cosine - second_half * sine_tab,
            first_half * sine_tab + second_half * cosine,
        ],
        axis=-1,
    )


def gather_dp(pack, dp):
    other = swapped(pack, "dp")
    return jnp.concatenate(
        [jnp.where(dp == 0, pack, other), jnp.where(dp == 0, other, pack)], axis=0
    )


def gather_plane(pair):
    mine = lax.all_gather(pair, PLANE, axis=0, tiled=True)
    return mine, swapped(mine, "core")


def scatter_rows(partial_rows, dp):
    part = lax.psum_scatter(partial_rows, PLANE, scatter_dimension=0, tiled=True)
    part = part.reshape(2, 32, part.shape[1])
    mine = lax.dynamic_index_in_dim(part, dp, 0, keepdims=False)
    theirs = lax.dynamic_index_in_dim(part, 1 - dp, 0, keepdims=False)
    return mine.astype(f32) + swapped(theirs, "dp").astype(f32)


def both_cores(own, sibling):
    return jnp.concatenate([own, sibling], axis=0)


def shards(
    hidden_in,
    prenorm,
    query_proj,
    latent_proj,
    midnorm,
    expand_proj,
    output_proj,
    postnorm,
    shared_gate,
    shared_up,
    shared_down,
    expert_gate,
    expert_up,
    expert_down,
    segments,
    routes,
    route_weights,
    cotangent,
):
    dp = lax.axis_index("dp")
    core = lax.axis_index("core")
    chip = lax.axis_index("y") * 4 + lax.axis_index("z")
    tok = hidden_in.shape[0]
    heads = query_proj.shape[1] // (QN + QR)
    half = D // 2
    expert_pos = chip * 2 + core
    score_scale = 1.0 / math.sqrt(QN + QR)

    gains = jnp.stack([prenorm, postnorm, jnp.pad(midnorm, (0, 24))], axis=1)
    pack_a = jnp.concatenate(
        [query_proj, latent_proj, jnp.pad(gains, ((0, 0), (0, 61)))], axis=1
    )
    pack_b = jnp.concatenate([expand_proj.reshape(32, 512), output_proj.T], axis=1)
    pack_c = jnp.concatenate([shared_gate, shared_up, shared_down.T], axis=1)
    own_a, sib_a = gather_plane(gather_dp(pack_a, dp))
    own_b, sib_b = gather_plane(gather_dp(pack_b, dp))
    own_c, sib_c = gather_plane(gather_dp(pack_c, dp))

    place = jnp.arange(D, dtype=jnp.int32)
    true_of = (
        (place // 32 % 2) * 1024
        + (place // 64 % 16) * 64
        + ((place // 1024) ^ core) * 32
        + place % 32
    )
    perm = (place[:, None] == true_of[None, :]).astype(bf16)
    place_l = jnp.arange(LATENT, dtype=jnp.int32)
    true_l = (
        (place_l // 8 % 2) * 256
        + (place_l // 16 % 16) * 16
        + ((place_l // 256) ^ core) * 8
        + place_l % 8
    )
    perm_l = (place_l[:, None] == true_l[None, :]).astype(bf16)
    mid_true = (
        (place // 32 % 2) * 256
        + (place // 64 % 16) * 16
        + ((place // 1024) ^ core) * 8
        + place % 32
    )
    perm_m = (
        (mid_true[:, None] == place_l[None, :]) & (place % 32 < 8)[:, None]
    ).astype(bf16)

    def unpermute(values):
        high, low = split_low(values)
        return matmul_nt(high, perm) + matmul_nt(low, perm)

    inputs = matmul(hidden_in, perm)
    upstream = matmul(cotangent, perm)
    up_low = upstream.astype(bf16)

    expert_ids = jnp.arange(32, dtype=jnp.int32)
    hits = routes[:, :, None] == expert_ids[None, None, :]
    named = jnp.sum(hits.astype(f32), axis=1)
    weight_te = jnp.sum(jnp.where(hits, route_weights[:, :, None], 0.0), axis=1)
    order = jnp.arange(tok, dtype=jnp.int32)
    earlier = (order[:, None] > order[None, :]).astype(bf16)
    rank = matmul(earlier, named.astype(bf16))
    rank_et = jnp.where(named > 0.5, rank, -1.0).T
    slot_ids = jnp.arange(SLOTS, dtype=jnp.int32).astype(f32)
    taken = rank_et[:, None, :] == slot_ids[None, :, None]
    slot_pick = taken.astype(bf16).reshape(32 * SLOTS, tok)
    slot_weight = jnp.where(taken, weight_te.T[:, None, :], 0.0).reshape(32 * SLOTS, tok)
    weight_hi, weight_lo = split_low(slot_weight)

    def exchange(rows):
        blocks = rows.reshape(32, SLOTS, D)
        return lax.all_to_all(blocks, EXPERT, split_axis=0, concat_axis=0, tiled=True).reshape(
            32 * SLOTS, D
        )

    grad_send = (matmul(weight_hi, cotangent) + matmul(weight_lo, cotangent)).astype(bf16)
    grad_rows = exchange(grad_send)

    pick = jnp.eye(8, 64, dtype=bf16)
    gain_rows = jnp.concatenate(
        [matmul_nt(pick, own_a[:, 2112:]), matmul_nt(pick, sib_a[:, 2112:])], axis=1
    )
    gain_one = gain_rows[0]
    gain_two = gain_rows[1]
    gain_mid = matmul(gain_rows.astype(bf16), perm_m)[2]

    normed_one, inverse_one = rms_forward(inputs, gain_one)
    h_one = normed_one.astype(bf16)
    projected = matmul(h_one[:, :half], own_a) + matmul(h_one[:, half:], sib_a)
    queries = projected[:, : heads * (QN + QR)].reshape(tok, heads, QN + QR)
    kv_pre = projected[:, heads * (QN + QR) : heads * (QN + QR) + LATENT + QR]
    q_nope = queries[:, :, :QN].astype(bf16)
    latent_raw = kv_pre[:, :LATENT]
    latent_normed, inverse_mid = rms_forward(latent_raw, gain_mid)
    positions = (expert_pos * tok + jnp.arange(tok, dtype=jnp.int32)).astype(f32)
    cosine, sine_tab = rope_tables(positions, QR)
    latent = jnp.concatenate(
        [latent_normed, rotate(kv_pre[:, LATENT:], cosine, sine_tab)], axis=1
    ).astype(bf16)
    expand_rows = jnp.concatenate([own_b[:, :512], sib_b[:, :512]], axis=0)
    w_expand = matmul(perm_l, expand_rows.reshape(LATENT, heads * (QN + DV))).astype(bf16)
    w_heads = w_expand.reshape(LATENT, heads, QN + DV)
    w_key = w_heads[:, :, :QN]
    w_value = w_heads[:, :, QN:]
    w_out_own = own_b[:, 512:]
    w_out_sib = sib_b[:, 512:]
    q_latent = jnp.einsum("thn,chn->thc", q_nope, w_key, preferred_element_type=f32)
    q_rotated = rotate(queries[:, :, QN:], cosine[:, None, :], sine_tab[:, None, :])
    q_full = jnp.concatenate([q_latent, q_rotated], axis=2).astype(bf16)

    own_blocks = jnp.stack([chip_shift(latent, k) for k in (4, 3, 2, 1)] + [latent])
    sib_blocks = swapped(
        lax.dynamic_slice_in_dim(own_blocks, 1 - core, 4, 0), "core"
    )
    window = jnp.concatenate([own_blocks, sib_blocks], axis=0).reshape(9 * tok, LATENT + QR)
    block_chip = jnp.concatenate(
        [chip - 4 + jnp.arange(5, dtype=jnp.int32), chip - 4 + core + jnp.arange(4, dtype=jnp.int32)]
    )
    block_core = jnp.concatenate(
        [jnp.full((5,), core, jnp.int32), jnp.full((4,), 1 - core, jnp.int32)]
    )
    block_id = block_chip * 2 + block_core
    seg_blocks = lax.dynamic_slice_in_dim(segments.reshape(2, 32, tok), dp, 1, 0)[0]
    chosen = jnp.arange(32, dtype=jnp.int32)[None, :, None] == block_id[:, None, None]
    seg_keys = jnp.sum(jnp.where(chosen, seg_blocks[None] + 1, 0), axis=1).reshape(9 * tok) - 1
    seg_query = lax.dynamic_index_in_dim(seg_blocks, expert_pos, 0, keepdims=False)
    key_pos = (block_id[:, None] * tok + jnp.arange(tok, dtype=jnp.int32)[None, :]).reshape(9 * tok)
    query_pos = expert_pos * tok + jnp.arange(tok, dtype=jnp.int32)
    offsets = query_pos[:, None] - key_pos[None, :]
    visible = (seg_query[:, None] == seg_keys[None, :]) & (offsets >= 0) & (offsets < WIN)

    def score_block():
        raw = jnp.einsum("thc,kc->htk", q_full, window, preferred_element_type=f32) * score_scale
        return jnp.where(visible[None], raw, neg_big)

    logits = score_block()
    row_max = jnp.max(logits, axis=2, keepdims=True)
    expo_vals = jnp.exp(logits - row_max)
    expo_sum = jnp.sum(expo_vals, axis=2, keepdims=True)
    log_total = row_max + jnp.log(expo_sum)
    probs_low = (expo_vals / expo_sum).astype(bf16)
    o_latent = jnp.einsum(
        "htk,kc->thc", probs_low, window[:, :LATENT], preferred_element_type=f32
    ).astype(bf16)
    o_heads = (
        jnp.einsum("thc,chv->thv", o_latent, w_value, preferred_element_type=f32)
        .astype(bf16)
        .reshape(tok, heads * DV)
    )
    attention = pair_sum(
        jnp.concatenate([matmul_nt(o_heads, w_out_own), matmul_nt(o_heads, w_out_sib)], axis=1),
        "tensor",
    )
    mid = inputs + attention
    normed_two, inverse_two = rms_forward(mid, gain_two)
    h_two = normed_two.astype(bf16)

    h_two_true = matmul_nt(h_two, perm).astype(bf16)
    expert_rows = exchange(matmul(slot_pick, h_two_true).astype(bf16))

    fs = shared_gate.shape[1]
    s_both = matmul(h_two[:, :half], own_c[:, : 2 * fs]) + matmul(h_two[:, half:], sib_c[:, : 2 * fs])
    s_gate = s_both[:, :fs]
    s_up = s_both[:, fs:]
    s_sig = jax.nn.sigmoid(s_gate)
    s_active = s_gate * s_sig
    s_hidden = (s_active * s_up).astype(bf16)
    s_part = jnp.concatenate(
        [matmul_nt(s_hidden, own_c[:, 2 * fs :]), matmul_nt(s_hidden, sib_c[:, 2 * fs :])], axis=1
    )
    back_shidden = matmul(up_low[:, :half], own_c[:, 2 * fs :]) + matmul(
        up_low[:, half:], sib_c[:, 2 * fs :]
    )
    back_sgate = (back_shidden * s_up * s_sig * (1.0 + s_gate * (1.0 - s_sig))).astype(bf16)
    back_sup = (back_shidden * s_active).astype(bf16)
    back_sboth = jnp.concatenate([back_sgate, back_sup], axis=1)
    shared_back = jnp.concatenate(
        [matmul_nt(back_sboth, own_c[:, : 2 * fs]), matmul_nt(back_sboth, sib_c[:, : 2 * fs])], axis=1
    )
    h_two_pair = both_cores(h_two[:, :half], swapped(h_two[:, half:], "core"))
    up_pair = both_cores(up_low[:, :half], swapped(up_low[:, half:], "core"))
    s_acts = jnp.concatenate([back_sboth, s_hidden], axis=1)
    s_pair = both_cores(s_acts, swapped(s_acts, "core"))
    shared_rows = jnp.concatenate(
        [matmul_tn(h_two_pair, s_pair[:, : 2 * fs]), matmul_tn(up_pair, s_pair[:, 2 * fs :])], axis=1
    ).astype(bf16)
    shared_grads = scatter_rows(shared_rows, dp)

    gate_pre = matmul(expert_rows, expert_gate[0])
    up_pre = matmul(expert_rows, expert_up[0])
    gate_sig = jax.nn.sigmoid(gate_pre)
    active = gate_pre * gate_sig
    hidden = (active * up_pre).astype(bf16)
    back_hidden = matmul_nt(grad_rows, expert_down[0])
    back_gate = (back_hidden * up_pre * gate_sig * (1.0 + gate_pre * (1.0 - gate_sig))).astype(bf16)
    back_up = (back_hidden * active).astype(bf16)
    row_grad = (matmul_nt(back_gate, expert_gate[0]) + matmul_nt(back_up, expert_up[0])).astype(bf16)
    row_back = exchange(row_grad)
    e_part = matmul(hidden, expert_down[0]).astype(bf16)
    e_part, row_back = lax.optimization_barrier((e_part, row_back))
    returned = exchange(e_part)
    expert_grads = tuple(
        pair_sum(g, "dp")
        for g in (
            matmul_tn(expert_rows, back_gate),
            matmul_tn(expert_rows, back_up),
            matmul_tn(hidden, grad_rows),
        )
    )
    routed = matmul_tn(weight_hi, returned) + matmul_tn(weight_lo, returned)
    output = unpermute(mid) + pair_sum(unpermute(s_part) + routed, "tensor")

    back_routed = matmul(matmul_tn(slot_pick, row_back).astype(bf16), perm)
    back_two = pair_sum(shared_back + back_routed, "tensor")
    back_midnorm, grad_gain_two = rms_backward(mid, inverse_two, gain_two, back_two)
    back_mid = upstream + back_midnorm
    back_attn = back_mid.astype(bf16)

    back_heads = (
        (matmul(back_attn[:, :half], w_out_own) + matmul(back_attn[:, half:], w_out_sib))
        .astype(bf16)
        .reshape(tok, heads, DV)
    )
    grad_value = jnp.einsum("thc,thv->chv", o_latent, back_heads, preferred_element_type=f32)
    back_olatent = jnp.einsum(
        "thv,chv->thc", back_heads, w_value, preferred_element_type=f32
    ).astype(bf16)
    probs_back = jnp.exp(score_block() - log_total)
    back_probs = jnp.einsum(
        "thc,kc->htk", back_olatent, window[:, :LATENT], preferred_element_type=f32
    )
    row_delta = jnp.sum(probs_back * back_probs, axis=2, keepdims=True)
    back_scores = (probs_back * (back_probs - row_delta) * score_scale).astype(bf16)
    back_qfull = jnp.einsum("htk,kc->thc", back_scores, window, preferred_element_type=f32)
    value_part = jnp.einsum(
        "htk,thc->kc", probs_back.astype(bf16), back_olatent, preferred_element_type=f32
    )
    back_window = jnp.einsum("htk,thc->kc", back_scores, q_full, preferred_element_type=f32)
    back_window = back_window + jnp.pad(value_part, ((0, 0), (0, QR)))
    back_blocks = back_window.reshape(9, tok, LATENT + QR)
    from_sib = swapped(back_blocks[5:].astype(bf16), "core").astype(f32)
    pad_block = jnp.zeros((1, tok, LATENT + QR), f32)
    from_sib = jnp.where(
        core == 0,
        jnp.concatenate([pad_block, from_sib], axis=0),
        jnp.concatenate([from_sib, pad_block], axis=0),
    )
    chip_blocks = back_blocks[:5] + from_sib
    back_latent = chip_blocks[4]
    for index, k in enumerate((4, 3, 2, 1)):
        back_latent = back_latent + chip_shift(chip_blocks[index].astype(bf16), -k).astype(f32)

    back_qlatent = back_qfull[:, :, :LATENT].astype(bf16)
    back_qrope = rotate(back_qfull[:, :, LATENT:], cosine[:, None, :], -sine_tab[:, None, :])
    grad_key = jnp.einsum("thc,thn->chn", back_qlatent, q_nope, preferred_element_type=f32)
    back_qnope = jnp.einsum("thc,chn->thn", back_qlatent, w_key, preferred_element_type=f32)
    back_queries = (
        jnp.concatenate([back_qnope, back_qrope], axis=2)
        .reshape(tok, heads * (QN + QR))
        .astype(bf16)
    )
    grad_expand = jnp.concatenate([grad_key, grad_value], axis=2).reshape(
        LATENT, heads * (QN + DV)
    )

    back_raw, grad_gain_mid = rms_backward(
        latent_raw, inverse_mid, gain_mid, back_latent[:, :LATENT]
    )
    back_kvpre = jnp.concatenate(
        [back_raw, rotate(back_latent[:, LATENT:], cosine, -sine_tab)], axis=1
    ).astype(bf16)
    back_both = jnp.concatenate(
        [back_queries, back_kvpre, jnp.zeros((tok, 64), bf16)], axis=1
    )
    back_one = pair_sum(
        jnp.concatenate([matmul_nt(back_both, own_a), matmul_nt(back_both, sib_a)], axis=1),
        "tensor",
    )
    back_innorm, grad_gain_one = rms_backward(inputs, inverse_one, gain_one, back_one)
    input_grad = unpermute(back_mid + back_innorm)

    h_one_pair = both_cores(h_one[:, :half], swapped(h_one[:, half:], "core"))
    attn_pair = both_cores(back_attn[:, :half], swapped(back_attn[:, half:], "core"))
    heads_pair = both_cores(o_heads, swapped(o_heads, "core"))
    back_pair = both_cores(back_both[:, :2112], swapped(back_both[:, :2112], "core"))
    rows_ql = matmul_tn(h_one_pair, back_pair)
    rows_out = matmul_tn(attn_pair, heads_pair)
    expand_low = matmul_tn(perm_l, grad_expand.astype(bf16)).astype(bf16)
    rows_expand = expand_low[:256].astype(f32) + swapped(expand_low[256:], "core").astype(f32)
    rows_expand = rows_expand.reshape(1024, 512)
    mid_low = matmul_nt(perm_m, grad_gain_mid.astype(bf16)[None, :])
    gain_cols = jnp.concatenate([grad_gain_one[:, None], grad_gain_two[:, None], mid_low], axis=1)
    gain_low = gain_cols.astype(bf16)
    rows_gain = gain_low[:half].astype(f32) + swapped(gain_low[half:], "core").astype(f32)
    attn_rows = jnp.concatenate(
        [rows_ql, jnp.pad(rows_gain, ((0, 0), (0, 61))), rows_expand, rows_out], axis=1
    ).astype(bf16)
    attn_grads = scatter_rows(attn_rows, dp)
    latent_gain = attn_grads[:, 1536:2176]
    replicated = latent_gain.at[:, 577].multiply(0.5).at[:, 576].multiply(0.5)
    replicated = pair_sum(replicated, "tensor")

    return (
        output.astype(bf16),
        input_grad,
        replicated[:, 576],
        attn_grads[:, :1536],
        replicated[:, :576],
        replicated[:8, 578],
        attn_grads[:, 2176:2688].reshape(8, 2048),
        attn_grads[:, 2688:].T,
        replicated[:, 577],
        shared_grads[:, :fs],
        shared_grads[:, fs : 2 * fs],
        shared_grads[:, 2 * fs :].T,
        expert_grads[0][None],
        expert_grads[1][None],
        expert_grads[2][None],
    )


def solution(mesh):
    fine = Mesh(
        mesh.devices.reshape(2, 4, 4, 2, 2), ("dp", "y", "z", "core", "tensor")
    )
    rows = ("dp", "y", "z", "core")
    placed = (
        P(rows, None),
        P(rows),
        P(rows, "tensor"),
        P(rows, None),
        P(rows),
        P(rows, "tensor"),
        P("tensor", rows),
        P(rows),
        P(rows, "tensor"),
        P(rows, "tensor"),
        P("tensor", rows),
        P(EXPERT, None, "tensor"),
        P(EXPERT, None, "tensor"),
        P(EXPERT, "tensor", None),
        P(),
        P(rows, None),
        P(rows, None),
        P(rows, None),
    )
    return jax.shard_map(
        shards,
        mesh=fine,
        in_specs=placed,
        out_specs=(
            P(rows, None),
            P(rows, None),
            P(rows),
            P(rows, "tensor"),
            P(rows, None),
            P(rows),
            P(rows, "tensor"),
            P("tensor", rows),
            P(rows),
            P(rows, "tensor"),
            P(rows, "tensor"),
            P("tensor", rows),
            P(EXPERT, None, "tensor"),
            P(EXPERT, None, "tensor"),
            P(EXPERT, "tensor", None),
        ),
        check_vma=False,
    )
```

```python
import functools
import math

import jax
import jax.numpy as jnp
from jax import lax
from jax.experimental import pallas as pl
from jax.experimental.pallas import tpu as pltpu
from jax.sharding import Mesh, PartitionSpec as P

D = 2048
QN = 128
QR = 64
DV = 128
LATENT = 512
TOPK = 6
WIN = 1024
SLOTS = 32

epsilon = 1e-06
neg_big = -1e30
f32 = jnp.float32
bf16 = jnp.bfloat16
PLANE = ("y", "z")
EXPERT = ("y", "z", "core")


def swapped(block, axis):
    return lax.ppermute(block, axis, [(0, 1), (1, 0)])


def chip_shift(block, distance):
    chips = range(16)
    route = [(i - distance, i) for i in chips if i - distance in chips]
    return lax.ppermute(block, PLANE, route)


def matmul(left_op, right_op):
    return jnp.dot(left_op, right_op, preferred_element_type=f32)


def matmul_tn(left_op, right_op):
    return lax.dot_general(
        left_op, right_op, (((0,), (0,)), ((), ())), preferred_element_type=f32
    )


def matmul_nt(left_op, right_op):
    return lax.dot_general(
        left_op, right_op, (((1,), (1,)), ((), ())), preferred_element_type=f32
    )


def pair_sum(part, axis):
    low = lax.optimization_barrier(part.astype(bf16))
    return low.astype(f32) + swapped(low, axis).astype(f32)


def split_low(values):
    high = values.astype(bf16)
    return high, (values - high.astype(f32)).astype(bf16)


def rms_forward(values, gain_vec):
    inverse = lax.rsqrt(jnp.mean(values * values, axis=-1, keepdims=True) + epsilon)
    return (values * inverse * gain_vec, inverse)


def rms_backward(values, inverse, gain_vec, upstream):
    scaled = upstream * gain_vec
    inner_mean = jnp.mean(scaled * values, axis=-1, keepdims=True)
    back_values = inverse * (scaled - values * inner_mean * inverse * inverse)
    gain_grad = jnp.sum(upstream * values * inverse, axis=0)
    return (back_values, gain_grad)


def rope_tables(positions, width):
    half_width = width // 2
    frequency = jnp.exp(
        -math.log(10000.0) * jnp.arange(half_width, dtype=f32) * (2.0 / width)
    )
    angles = positions[:, None] * frequency[None, :]
    return (jnp.cos(angles), jnp.sin(angles))


def rotate(values, cosine, sine_tab):
    half_width = values.shape[-1] // 2
    first_half = values[..., :half_width]
    second_half = values[..., half_width:]
    return jnp.concatenate(
        [
            first_half * cosine - second_half * sine_tab,
            first_half * sine_tab + second_half * cosine,
        ],
        axis=-1,
    )


def gather_dp(pack, dp):
    other = swapped(pack, "dp")
    return jnp.concatenate(
        [jnp.where(dp == 0, pack, other), jnp.where(dp == 0, other, pack)], axis=0
    )


def gather_plane(pair):
    mine = lax.all_gather(pair, PLANE, axis=0, tiled=True)
    return mine, swapped(mine, "core")


def finish_rows(part, dp):
    part = part.reshape(2, 32, part.shape[1])
    mine = lax.dynamic_index_in_dim(part, dp, 0, keepdims=False)
    theirs = lax.dynamic_index_in_dim(part, 1 - dp, 0, keepdims=False)
    return mine.astype(f32) + swapped(theirs, "dp").astype(f32)


def both_cores(own, sibling):
    return jnp.concatenate([own, sibling], axis=0)


WIDE = 640
VMEM_BYTES = 48 * 1024 * 1024


def rope_places(head):
    row = lax.broadcasted_iota(jnp.int32, (512, 128), 0)
    lane = lax.broadcasted_iota(jnp.int32, (512, 128), 1)
    wanted = lax.shift_right_logical(lane, 5) * 256 + head * 32 + (lane & 31)
    return jnp.where((lane < 64) & (row == wanted), 1.0, 0.0).astype(bf16)


def attend_kernel(scale, qn_ref, rope_ref, w_ref, win_ref, bias_ref, qf_ref, ol_ref, oh_ref, lse_ref):
    q_latent = matmul_nt(qn_ref[...], w_ref[:, :QN]).astype(bf16)
    q_rope = matmul(rope_ref[...], rope_places(pl.program_id(0))).astype(bf16)
    qf_ref[0, :, :LATENT] = q_latent
    qf_ref[0, :, LATENT:] = q_rope
    scores = matmul_nt(q_latent, win_ref[:, :LATENT]) + matmul_nt(q_rope, win_ref[:, LATENT:])
    logits = scores * scale + bias_ref[...]
    row_max = jnp.max(logits, axis=1, keepdims=True)
    expo = jnp.exp(logits - row_max)
    total = jnp.sum(expo, axis=1, keepdims=True)
    probs = (expo / total).astype(bf16)
    o_latent = matmul(probs, win_ref[:, :LATENT]).astype(bf16)
    ol_ref[0] = o_latent
    oh_ref[...] = matmul(o_latent, w_ref[:, QN:]).astype(bf16)
    lse_ref[0] = jnp.broadcast_to(row_max + jnp.log(total), lse_ref.shape[1:])


def attend_back_kernel(
    scale,
    bh_ref,
    w_ref,
    win_ref,
    bias_ref,
    qf_ref,
    qn_ref,
    ol_ref,
    lse_ref,
    cos_ref,
    sin_ref,
    ge_ref,
    bqn_ref,
    rope_ref,
    bwin_ref,
):
    head = pl.program_id(0)

    @pl.when(head == 0)
    def _():
        bwin_ref[...] = jnp.zeros_like(bwin_ref)
        rope_ref[...] = jnp.zeros_like(rope_ref)

    back_heads = bh_ref[...]
    ge_ref[:, QN:] = matmul_tn(ol_ref[0], back_heads).astype(bf16)
    back_olatent = matmul_nt(back_heads, w_ref[:, QN:]).astype(bf16)
    scores = matmul_nt(qf_ref[0], win_ref[...])
    probs = jnp.exp(scores * scale + bias_ref[...] - lse_ref[0][:, :1])
    back_probs = matmul_nt(back_olatent, win_ref[:, :LATENT])
    delta = jnp.sum(probs * back_probs, axis=1, keepdims=True)
    back_scores = (probs * (back_probs - delta) * scale).astype(bf16)
    bwin_ref[...] += matmul_tn(back_scores, qf_ref[0])
    bwin_ref[:, :LATENT] += matmul_tn(probs.astype(bf16), back_olatent)
    back_q = matmul(back_scores, win_ref[...])
    back_qlatent = back_q[:, :LATENT].astype(bf16)
    ge_ref[:, :QN] = matmul_tn(back_qlatent, qn_ref[...]).astype(bf16)
    bqn_ref[...] = matmul(back_qlatent, w_ref[:, :QN]).astype(bf16)
    halves = back_q[:, LATENT:]
    lane = lax.broadcasted_iota(jnp.int32, halves.shape, 1)
    crossed = jnp.where(lane < 32, pltpu.roll(halves, 96, 1), pltpu.roll(halves, 32, 1))
    turned = (halves * cos_ref[...] + crossed * sin_ref[...]).astype(bf16)
    rope_ref[...] += matmul_nt(turned, rope_places(head)).astype(bf16)


def whole(shape):
    return pl.BlockSpec(shape, lambda h: (0,) * len(shape))


def attend(scale, q_nope, rope, w_expand, window, bias):
    tok, heads, keys = q_nope.shape[0], q_nope.shape[1] // QN, window.shape[0]
    return pl.pallas_call(
        functools.partial(attend_kernel, scale),
        grid=(heads,),
        in_specs=[
            pl.BlockSpec((tok, QN), lambda h: (0, h)),
            whole((tok, 512)),
            pl.BlockSpec((LATENT, QN + DV), lambda h: (0, h)),
            whole((keys, WIDE)),
            whole((tok, keys)),
        ],
        out_specs=[
            pl.BlockSpec((1, tok, WIDE), lambda h: (h, 0, 0)),
            pl.BlockSpec((1, tok, LATENT), lambda h: (h, 0, 0)),
            pl.BlockSpec((tok, DV), lambda h: (0, h)),
            pl.BlockSpec((1, tok, 128), lambda h: (h, 0, 0)),
        ],
        out_shape=[
            jax.ShapeDtypeStruct((heads, tok, WIDE), bf16),
            jax.ShapeDtypeStruct((heads, tok, LATENT), bf16),
            jax.ShapeDtypeStruct((tok, heads * DV), bf16),
            jax.ShapeDtypeStruct((heads, tok, 128), f32),
        ],
        compiler_params=pltpu.CompilerParams(vmem_limit_bytes=VMEM_BYTES),
        cost_estimate=pl.CostEstimate(
            flops=heads * tok * keys * 2400, bytes_accessed=12 << 20, transcendentals=heads * tok * keys
        ),
        name="attend",
    )(q_nope, rope, w_expand, window, bias)


def attend_back(scale, back_heads, w_expand, window, bias, q_full, q_nope, o_latent, log_total, cos, sin):
    tok, heads, keys = q_nope.shape[0], q_nope.shape[1] // QN, window.shape[0]
    return pl.pallas_call(
        functools.partial(attend_back_kernel, scale),
        grid=(heads,),
        in_specs=[
            pl.BlockSpec((tok, DV), lambda h: (0, h)),
            pl.BlockSpec((LATENT, QN + DV), lambda h: (0, h)),
            whole((keys, WIDE)),
            whole((tok, keys)),
            pl.BlockSpec((1, tok, WIDE), lambda h: (h, 0, 0)),
            pl.BlockSpec((tok, QN), lambda h: (0, h)),
            pl.BlockSpec((1, tok, LATENT), lambda h: (h, 0, 0)),
            pl.BlockSpec((1, tok, 128), lambda h: (h, 0, 0)),
            whole((tok, 128)),
            whole((tok, 128)),
        ],
        out_specs=[
            pl.BlockSpec((LATENT, QN + DV), lambda h: (0, h)),
            pl.BlockSpec((tok, QN), lambda h: (0, h)),
            whole((tok, 512)),
            whole((keys, WIDE)),
        ],
        out_shape=[
            jax.ShapeDtypeStruct((LATENT, heads * (QN + DV)), bf16),
            jax.ShapeDtypeStruct((tok, heads * QN), bf16),
            jax.ShapeDtypeStruct((tok, 512), bf16),
            jax.ShapeDtypeStruct((keys, WIDE), f32),
        ],
        compiler_params=pltpu.CompilerParams(vmem_limit_bytes=VMEM_BYTES),
        cost_estimate=pl.CostEstimate(
            flops=heads * tok * keys * 6400, bytes_accessed=20 << 20, transcendentals=heads * tok * keys
        ),
        name="attend_back",
    )(back_heads, w_expand, window, bias, q_full, q_nope, o_latent, log_total, cos, sin)


def shards(
    hidden_in,
    prenorm,
    query_proj,
    latent_proj,
    midnorm,
    expand_proj,
    output_proj,
    postnorm,
    shared_gate,
    shared_up,
    shared_down,
    expert_gate,
    expert_up,
    expert_down,
    segments,
    routes,
    route_weights,
    cotangent,
):
    dp = lax.axis_index("dp")
    core = lax.axis_index("core")
    chip = lax.axis_index("y") * 4 + lax.axis_index("z")
    tok = hidden_in.shape[0]
    heads = query_proj.shape[1] // (QN + QR)
    half = D // 2
    expert_pos = chip * 2 + core
    score_scale = 1.0 / math.sqrt(QN + QR)

    gains = jnp.stack([prenorm, postnorm, jnp.pad(midnorm, (0, 24))], axis=1)
    q_cols = query_proj.reshape(32, heads, QN + QR)
    l_cols = latent_proj[:, :LATENT].reshape(32, 2, 16, 2, 8).transpose(0, 3, 2, 1, 4)
    pack_a = jnp.concatenate(
        [
            q_cols[:, :, :QN].reshape(32, heads * QN),
            q_cols[:, :, QN : QN + 32].reshape(32, heads * 32),
            q_cols[:, :, QN + 32 :].reshape(32, heads * 32),
            l_cols.reshape(32, LATENT),
            latent_proj[:, LATENT:],
            jnp.pad(gains, ((0, 0), (0, 61))),
        ],
        axis=1,
    )
    pack_b = jnp.concatenate([expand_proj.reshape(32, 512), output_proj.T], axis=1)
    pack_c = jnp.concatenate([shared_gate, shared_up, shared_down.T], axis=1)
    own_a, sib_a = gather_plane(gather_dp(pack_a, dp))
    own_b, sib_b = gather_plane(gather_dp(pack_b, dp))

    place = jnp.arange(D, dtype=jnp.int32)
    true_of = (
        (place // 32 % 2) * 1024
        + (place // 64 % 16) * 64
        + ((place // 1024) ^ core) * 32
        + place % 32
    )
    perm = (place[:, None] == true_of[None, :]).astype(bf16)
    place_l = jnp.arange(LATENT, dtype=jnp.int32)
    mid_at = ((place // 1024) ^ core) * 256 + (place // 32 % 32) * 8 + place % 32
    perm_m = ((mid_at[:, None] == place_l[None, :]) & (place % 32 < 8)[:, None]).astype(bf16)

    def unpermute(values):
        high, low = split_low(values)
        return matmul_nt(high, perm) + matmul_nt(low, perm)

    inputs = matmul(hidden_in, perm)
    upstream = matmul(cotangent, perm)
    up_low = upstream.astype(bf16)

    expert_ids = jnp.arange(32, dtype=jnp.int32)
    hits = routes[:, :, None] == expert_ids[None, None, :]
    named = jnp.sum(hits.astype(f32), axis=1)
    weight_te = jnp.sum(jnp.where(hits, route_weights[:, :, None], 0.0), axis=1)
    order = jnp.arange(tok, dtype=jnp.int32)
    earlier = (order[:, None] > order[None, :]).astype(bf16)
    rank = matmul(earlier, named.astype(bf16))
    rank_et = jnp.where(named > 0.5, rank, -1.0).T
    slot_ids = jnp.arange(SLOTS, dtype=jnp.int32).astype(f32)
    taken = rank_et[:, None, :] == slot_ids[None, :, None]
    slot_pick = taken.astype(bf16).reshape(32 * SLOTS, tok)
    slot_weight = jnp.where(taken, weight_te.T[:, None, :], 0.0).reshape(32 * SLOTS, tok)
    weight_hi, weight_lo = split_low(slot_weight)

    def exchange(rows):
        blocks = rows.reshape(32, SLOTS, D)
        return lax.all_to_all(blocks, EXPERT, split_axis=0, concat_axis=0, tiled=True).reshape(
            32 * SLOTS, D
        )

    grad_send = (matmul(weight_hi, cotangent) + matmul(weight_lo, cotangent)).astype(bf16)
    grad_rows = exchange(grad_send)
    own_b, sib_b, grad_rows = lax.optimization_barrier((own_b, sib_b, grad_rows))
    pack_c, own_a = lax.optimization_barrier((pack_c, own_a))
    own_c, sib_c = gather_plane(gather_dp(pack_c, dp))

    pick = jnp.eye(8, 64, dtype=bf16)
    gain_rows = jnp.concatenate(
        [matmul_nt(pick, own_a[:, 2112:]), matmul_nt(pick, sib_a[:, 2112:])], axis=1
    )
    gain_one = gain_rows[0]
    gain_two = gain_rows[1]
    gain_mid = matmul(gain_rows.astype(bf16), perm_m)[2]

    normed_one, inverse_one = rms_forward(inputs, gain_one)
    h_one = normed_one.astype(bf16)
    projected = matmul(h_one[:, :half], own_a) + matmul(h_one[:, half:], sib_a)
    q_nope = projected[:, : heads * QN].astype(bf16)
    q_first = projected[:, 1024:1280]
    q_second = projected[:, 1280:1536]
    kv_pre = projected[:, 1536:2112]
    latent_raw = kv_pre[:, :LATENT]
    latent_normed, inverse_mid = rms_forward(latent_raw, gain_mid)
    positions = (expert_pos * tok + jnp.arange(tok, dtype=jnp.int32)).astype(f32)
    cosine, sine_tab = rope_tables(positions, QR)
    latent = jnp.concatenate(
        [
            latent_normed,
            rotate(kv_pre[:, LATENT:], cosine, sine_tab),
            jnp.zeros((tok, WIDE - LATENT - QR), f32),
        ],
        axis=1,
    ).astype(bf16)
    cos_all = jnp.tile(cosine, (1, heads))
    sin_all = jnp.tile(sine_tab, (1, heads))
    rope = jnp.concatenate(
        [q_first * cos_all - q_second * sin_all, q_first * sin_all + q_second * cos_all], axis=1
    ).astype(bf16)
    own_x = own_b[:, :512].reshape(256, heads * (QN + DV))
    sib_x = sib_b[:, :512].reshape(256, heads * (QN + DV))
    w_expand = jnp.concatenate(
        [jnp.where(core == 0, own_x, sib_x), jnp.where(core == 0, sib_x, own_x)], axis=0
    )
    w_out_own = own_b[:, 512:]
    w_out_sib = sib_b[:, 512:]

    own_blocks = jnp.stack([chip_shift(latent, k) for k in (4, 3, 2, 1)] + [latent])
    sib_blocks = swapped(
        lax.dynamic_slice_in_dim(own_blocks, 1 - core, 4, 0), "core"
    )
    window = jnp.concatenate([own_blocks, sib_blocks], axis=0).reshape(9 * tok, WIDE)
    block_chip = jnp.concatenate(
        [chip - 4 + jnp.arange(5, dtype=jnp.int32), chip - 4 + core + jnp.arange(4, dtype=jnp.int32)]
    )
    block_core = jnp.concatenate(
        [jnp.full((5,), core, jnp.int32), jnp.full((4,), 1 - core, jnp.int32)]
    )
    block_id = block_chip * 2 + block_core
    seg_blocks = lax.dynamic_slice_in_dim(segments.reshape(2, 32, tok), dp, 1, 0)[0]
    chosen = jnp.arange(32, dtype=jnp.int32)[None, :, None] == block_id[:, None, None]
    seg_keys = jnp.sum(jnp.where(chosen, seg_blocks[None] + 1, 0), axis=1).reshape(9 * tok) - 1
    seg_query = lax.dynamic_index_in_dim(seg_blocks, expert_pos, 0, keepdims=False)
    key_pos = (block_id[:, None] * tok + jnp.arange(tok, dtype=jnp.int32)[None, :]).reshape(9 * tok)
    query_pos = expert_pos * tok + jnp.arange(tok, dtype=jnp.int32)
    offsets = query_pos[:, None] - key_pos[None, :]
    visible = (seg_query[:, None] == seg_keys[None, :]) & (offsets >= 0) & (offsets < WIN)

    bias = jnp.where(visible, 0.0, neg_big)
    q_full, o_latent, o_heads, log_total = attend(
        score_scale, q_nope, rope, w_expand, window, bias
    )
    attention = pair_sum(
        jnp.concatenate([matmul_nt(o_heads, w_out_own), matmul_nt(o_heads, w_out_sib)], axis=1),
        "tensor",
    )
    mid = inputs + attention
    normed_two, inverse_two = rms_forward(mid, gain_two)
    h_two = normed_two.astype(bf16)

    h_two_true = matmul_nt(h_two, perm).astype(bf16)
    expert_rows = exchange(matmul(slot_pick, h_two_true).astype(bf16))

    fs = shared_gate.shape[1]
    s_both = matmul(h_two[:, :half], own_c[:, : 2 * fs]) + matmul(h_two[:, half:], sib_c[:, : 2 * fs])
    s_gate = s_both[:, :fs]
    s_up = s_both[:, fs:]
    s_sig = jax.nn.sigmoid(s_gate)
    s_active = s_gate * s_sig
    s_hidden = (s_active * s_up).astype(bf16)
    s_part = jnp.concatenate(
        [matmul_nt(s_hidden, own_c[:, 2 * fs :]), matmul_nt(s_hidden, sib_c[:, 2 * fs :])], axis=1
    )
    back_shidden = matmul(up_low[:, :half], own_c[:, 2 * fs :]) + matmul(
        up_low[:, half:], sib_c[:, 2 * fs :]
    )
    back_sgate = (back_shidden * s_up * s_sig * (1.0 + s_gate * (1.0 - s_sig))).astype(bf16)
    back_sup = (back_shidden * s_active).astype(bf16)
    back_sboth = jnp.concatenate([back_sgate, back_sup], axis=1)
    shared_back = jnp.concatenate(
        [matmul_nt(back_sboth, own_c[:, : 2 * fs]), matmul_nt(back_sboth, sib_c[:, : 2 * fs])], axis=1
    )
    h_two_pair = both_cores(h_two[:, :half], swapped(h_two[:, half:], "core"))
    up_pair = both_cores(up_low[:, :half], swapped(up_low[:, half:], "core"))
    s_acts = jnp.concatenate([back_sboth, s_hidden], axis=1)
    s_pair = both_cores(s_acts, swapped(s_acts, "core"))
    shared_rows = jnp.concatenate(
        [matmul_tn(h_two_pair, s_pair[:, : 2 * fs]), matmul_tn(up_pair, s_pair[:, 2 * fs :])], axis=1
    ).astype(bf16)

    gate_pre = matmul(expert_rows, expert_gate[0])
    up_pre = matmul(expert_rows, expert_up[0])
    gate_sig = jax.nn.sigmoid(gate_pre)
    active = gate_pre * gate_sig
    hidden = (active * up_pre).astype(bf16)
    back_hidden = matmul_nt(grad_rows, expert_down[0])
    back_gate = (back_hidden * up_pre * gate_sig * (1.0 + gate_pre * (1.0 - gate_sig))).astype(bf16)
    back_up = (back_hidden * active).astype(bf16)
    row_grad = (matmul_nt(back_gate, expert_gate[0]) + matmul_nt(back_up, expert_up[0])).astype(bf16)
    row_back = exchange(row_grad)
    e_part = matmul(hidden, expert_down[0]).astype(bf16)
    expert_low = (
        matmul_tn(expert_rows, back_gate).astype(bf16),
        matmul_tn(expert_rows, back_up).astype(bf16),
        matmul_tn(hidden, grad_rows).astype(bf16),
    )
    row_back = lax.optimization_barrier((row_back, shared_rows, expert_low, shared_back))[0]
    shared_part = lax.psum_scatter(shared_rows, PLANE, scatter_dimension=0, tiled=True)
    expert_other = tuple(swapped(g, "dp") for g in expert_low)
    e_part = lax.optimization_barrier((e_part, row_back))[0]
    returned = exchange(e_part)
    back_routed = matmul(matmul_tn(slot_pick, row_back).astype(bf16), perm)
    back_two = pair_sum(shared_back + back_routed, "tensor")
    back_midnorm, grad_gain_two = rms_backward(mid, inverse_two, gain_two, back_two)
    back_mid = upstream + back_midnorm
    back_attn = back_mid.astype(bf16)
    first_other, back_attn = lax.optimization_barrier((expert_other[0], back_attn))

    back_heads = (
        matmul(back_attn[:, :half], w_out_own) + matmul(back_attn[:, half:], w_out_sib)
    ).astype(bf16)
    pad_lanes = jnp.zeros((tok, 64), f32)
    grad_expand, back_qnope, back_rope, back_window = attend_back(
        score_scale,
        back_heads,
        w_expand,
        window,
        bias,
        q_full,
        q_nope,
        o_latent,
        log_total,
        jnp.concatenate([cosine, cosine, pad_lanes], axis=1),
        jnp.concatenate([sine_tab, -sine_tab, pad_lanes], axis=1),
    )
    back_blocks = back_window.reshape(9, tok, WIDE)
    from_sib = swapped(back_blocks[5:].astype(bf16), "core").astype(f32)
    pad_block = jnp.zeros((1, tok, WIDE), f32)
    from_sib = jnp.where(
        core == 0,
        jnp.concatenate([pad_block, from_sib], axis=0),
        jnp.concatenate([from_sib, pad_block], axis=0),
    )
    chip_blocks = back_blocks[:5] + from_sib
    back_latent = chip_blocks[4]
    for index, k in enumerate((4, 3, 2, 1)):
        back_latent = back_latent + chip_shift(chip_blocks[index].astype(bf16), -k).astype(f32)

    back_queries = jnp.concatenate([back_qnope, back_rope], axis=1)

    back_raw, grad_gain_mid = rms_backward(
        latent_raw, inverse_mid, gain_mid, back_latent[:, :LATENT]
    )
    back_kvpre = jnp.concatenate(
        [back_raw, rotate(back_latent[:, LATENT : LATENT + QR], cosine, -sine_tab)], axis=1
    ).astype(bf16)
    shared_part, second_other, returned, back_queries = lax.optimization_barrier(
        (shared_part, expert_other[1], returned, back_queries)
    )
    back_both = jnp.concatenate(
        [back_queries, back_kvpre, jnp.zeros((tok, 64), bf16)], axis=1
    )
    back_one = pair_sum(
        jnp.concatenate([matmul_nt(back_both, own_a), matmul_nt(back_both, sib_a)], axis=1),
        "tensor",
    )
    back_innorm, grad_gain_one = rms_backward(inputs, inverse_one, gain_one, back_one)
    input_grad = unpermute(back_mid + back_innorm)

    routed = matmul_tn(weight_hi, returned) + matmul_tn(weight_lo, returned)
    output = unpermute(mid) + pair_sum(unpermute(s_part) + routed, "tensor")

    h_one_pair = both_cores(h_one[:, :half], swapped(h_one[:, half:], "core"))
    attn_pair = both_cores(back_attn[:, :half], swapped(back_attn[:, half:], "core"))
    heads_pair = both_cores(o_heads, swapped(o_heads, "core"))
    back_pair = both_cores(back_both[:, :2112], swapped(back_both[:, :2112], "core"))
    rows_ql = matmul_tn(h_one_pair, back_pair)
    rows_out = matmul_tn(attn_pair, heads_pair)
    expand_mine = lax.dynamic_slice_in_dim(grad_expand, core * 256, 256, 0)
    expand_theirs = lax.dynamic_slice_in_dim(grad_expand, 256 - core * 256, 256, 0)
    rows_expand = expand_mine.astype(f32) + swapped(expand_theirs, "core").astype(f32)
    rows_expand = rows_expand.reshape(1024, 512)
    mid_low = matmul_nt(perm_m, grad_gain_mid.astype(bf16)[None, :])
    gain_cols = jnp.concatenate([grad_gain_one[:, None], grad_gain_two[:, None], mid_low], axis=1)
    gain_low = gain_cols.astype(bf16)
    rows_gain = gain_low[:half].astype(f32) + swapped(gain_low[half:], "core").astype(f32)
    attn_rows = jnp.concatenate(
        [rows_ql, jnp.pad(rows_gain, ((0, 0), (0, 61))), rows_expand, rows_out], axis=1
    ).astype(bf16)
    attn_part = lax.psum_scatter(attn_rows, PLANE, scatter_dimension=0, tiled=True)
    attn_part, third_other = lax.optimization_barrier((attn_part, expert_other[2]))
    attn_grads = finish_rows(attn_part, dp)
    shared_grads = finish_rows(shared_part, dp)
    expert_grads = tuple(
        mine.astype(f32) + other.astype(f32)
        for mine, other in zip(expert_low, (first_other, second_other, third_other))
    )
    latent_gain = attn_grads[:, 1536:2176]
    replicated = latent_gain.at[:, 577].multiply(0.5).at[:, 576].multiply(0.5)
    replicated = pair_sum(replicated, "tensor")
    query_grad = jnp.concatenate(
        [
            attn_grads[:, :1024].reshape(32, heads, QN),
            attn_grads[:, 1024:1280].reshape(32, heads, 32),
            attn_grads[:, 1280:1536].reshape(32, heads, 32),
        ],
        axis=2,
    ).reshape(32, heads * (QN + QR))
    latent_cols = replicated[:, :LATENT].reshape(32, 2, 16, 2, 8).transpose(0, 3, 2, 1, 4)
    latent_grad = jnp.concatenate(
        [latent_cols.reshape(32, LATENT), replicated[:, LATENT : LATENT + QR]], axis=1
    )

    return (
        output.astype(bf16),
        input_grad,
        replicated[:, 576],
        query_grad,
        latent_grad,
        replicated[:8, 578],
        attn_grads[:, 2176:2688].reshape(8, 2048),
        attn_grads[:, 2688:].T,
        replicated[:, 577],
        shared_grads[:, :fs],
        shared_grads[:, fs : 2 * fs],
        shared_grads[:, 2 * fs :].T,
        expert_grads[0][None],
        expert_grads[1][None],
        expert_grads[2][None],
    )


def solution(mesh):
    fine = Mesh(
        mesh.devices.reshape(2, 4, 4, 2, 2), ("dp", "y", "z", "core", "tensor")
    )
    rows = ("dp", "y", "z", "core")
    placed = (
        P(rows, None),
        P(rows),
        P(rows, "tensor"),
        P(rows, None),
        P(rows),
        P(rows, "tensor"),
        P("tensor", rows),
        P(rows),
        P(rows, "tensor"),
        P(rows, "tensor"),
        P("tensor", rows),
        P(EXPERT, None, "tensor"),
        P(EXPERT, None, "tensor"),
        P(EXPERT, "tensor", None),
        P(),
        P(rows, None),
        P(rows, None),
        P(rows, None),
    )
    return jax.shard_map(
        shards,
        mesh=fine,
        in_specs=placed,
        out_specs=(
            P(rows, None),
            P(rows, None),
            P(rows),
            P(rows, "tensor"),
            P(rows, None),
            P(rows),
            P(rows, "tensor"),
            P("tensor", rows),
            P(rows),
            P(rows, "tensor"),
            P(rows, "tensor"),
            P("tensor", rows),
            P(EXPERT, None, "tensor"),
            P(EXPERT, None, "tensor"),
            P(EXPERT, "tensor", None),
        ),
        check_vma=False,
    )
```

```python
import functools
import math

import jax
import jax.numpy as jnp
from jax import lax
from jax.experimental import pallas as pl
from jax.experimental.pallas import tpu as pltpu
from jax.sharding import Mesh, PartitionSpec as P

D = 2048
QN = 128
QR = 64
DV = 128
LATENT = 512
TOPK = 6
WIN = 1024
SLOTS = 32

epsilon = 1e-06
neg_big = -1e30
f32 = jnp.float32
bf16 = jnp.bfloat16
PLANE = ("y", "z")
EXPERT = ("y", "z", "core")


def swapped(block, axis):
    return lax.ppermute(block, axis, [(0, 1), (1, 0)])


def chip_shift(block, distance):
    chips = range(16)
    route = [(i - distance, i) for i in chips if i - distance in chips]
    return lax.ppermute(block, PLANE, route)


def matmul(left_op, right_op):
    return jnp.dot(left_op, right_op, preferred_element_type=f32)


def matmul_tn(left_op, right_op):
    return lax.dot_general(
        left_op, right_op, (((0,), (0,)), ((), ())), preferred_element_type=f32
    )


def matmul_nt(left_op, right_op):
    return lax.dot_general(
        left_op, right_op, (((1,), (1,)), ((), ())), preferred_element_type=f32
    )


def pair_sum(part, axis):
    low = lax.optimization_barrier(part.astype(bf16))
    return low.astype(f32) + swapped(low, axis).astype(f32)


def split_low(values):
    high = values.astype(bf16)
    return high, (values - high.astype(f32)).astype(bf16)


def rms_forward(values, gain_vec):
    inverse = lax.rsqrt(jnp.mean(values * values, axis=-1, keepdims=True) + epsilon)
    return (values * inverse * gain_vec, inverse)


def rms_backward(values, inverse, gain_vec, upstream):
    scaled = upstream * gain_vec
    inner_mean = jnp.mean(scaled * values, axis=-1, keepdims=True)
    back_values = inverse * (scaled - values * inner_mean * inverse * inverse)
    gain_grad = jnp.sum(upstream * values * inverse, axis=0)
    return (back_values, gain_grad)


def rope_tables(positions, width):
    half_width = width // 2
    frequency = jnp.exp(
        -math.log(10000.0) * jnp.arange(half_width, dtype=f32) * (2.0 / width)
    )
    angles = positions[:, None] * frequency[None, :]
    return (jnp.cos(angles), jnp.sin(angles))


def rotate(values, cosine, sine_tab):
    half_width = values.shape[-1] // 2
    first_half = values[..., :half_width]
    second_half = values[..., half_width:]
    return jnp.concatenate(
        [
            first_half * cosine - second_half * sine_tab,
            first_half * sine_tab + second_half * cosine,
        ],
        axis=-1,
    )


def xored(block, axis, k):
    return lax.ppermute(block, axis, [(i, i ^ k) for i in range(4)])


def merged(own, other, upper, dim):
    return jnp.concatenate(
        [jnp.where(upper, other, own), jnp.where(upper, own, other)], axis=dim
    )


def joined(own, other, pos, cross, dim):
    if not cross:
        return merged(own, other, pos >= 2, dim)
    outer = (pos == 0) | (pos == 3)
    ends = jnp.where(outer, own, other)
    middle = jnp.where(outer, other, own)
    low, high = jnp.split(ends, 2, axis=dim)
    return jnp.concatenate([low, middle, high], axis=dim)


def together(*trees):
    return lax.optimization_barrier(trees)


def gather_step(blocks, axes, second):
    return [
        xored(block, axis, 1 if cross == second else 3)
        for block, (axis, _, _, cross) in zip(blocks, axes)
    ]


def steps_of(axis, cross):
    return ((axis, 3), (axis, 1)) if cross else ((axis, 1), (axis, 3))


def stream_places(size, first, cross, y_pos, z_pos):
    index = jnp.arange(size, dtype=jnp.int32)
    part = size // 16
    order = jnp.asarray((3, 2, 0, 1) if cross else (1, 2, 0, 3), jnp.int32)
    one, two = order[index // (4 * part)], index // part % 4
    y_at, z_at = (two, one ^ z_pos) if first == "z" else (one ^ y_pos, two)
    at = (y_at * 4 + z_at) * part + index % part
    return (index[:, None] == at[None, :]).astype(bf16)


def summed(mine, other, dim):
    return jnp.concatenate(mine, axis=dim).astype(f32) + jnp.concatenate(other, axis=dim).astype(f32)


def add_low(left, right):
    return (left.astype(f32) + right.astype(f32)).astype(bf16)


def gather_dp(pack, dp):
    other = swapped(pack, "dp")
    return jnp.concatenate(
        [jnp.where(dp == 0, pack, other), jnp.where(dp == 0, other, pack)], axis=0
    )


def mine_of(part, dp):
    return lax.dynamic_index_in_dim(part, dp, 0, keepdims=False)


def theirs_of(part, dp):
    return lax.dynamic_index_in_dim(part, 1 - dp, 0, keepdims=False)


def finish_rows(part, dp):
    part = part.reshape(2, 32, part.shape[1])
    mine = lax.dynamic_index_in_dim(part, dp, 0, keepdims=False)
    theirs = lax.dynamic_index_in_dim(part, 1 - dp, 0, keepdims=False)
    return mine.astype(f32) + swapped(theirs, "dp").astype(f32)


def both_cores(own, sibling):
    return jnp.concatenate([own, sibling], axis=0)


WIDE = 640
VMEM_BYTES = 48 * 1024 * 1024


def rope_places(head):
    row = lax.broadcasted_iota(jnp.int32, (512, 128), 0)
    lane = lax.broadcasted_iota(jnp.int32, (512, 128), 1)
    wanted = lax.shift_right_logical(lane, 5) * 256 + head * 32 + (lane & 31)
    return jnp.where((lane < 64) & (row == wanted), 1.0, 0.0).astype(bf16)


def attend_kernel(scale, qn_ref, rope_ref, w_ref, win_ref, bias_ref, qf_ref, ol_ref, oh_ref, lse_ref):
    q_latent = matmul_nt(qn_ref[...], w_ref[:, :QN]).astype(bf16)
    q_rope = matmul(rope_ref[...], rope_places(pl.program_id(0))).astype(bf16)
    qf_ref[0, :, :LATENT] = q_latent
    qf_ref[0, :, LATENT:] = q_rope
    scores = matmul_nt(q_latent, win_ref[:, :LATENT]) + matmul_nt(q_rope, win_ref[:, LATENT:])
    logits = scores * scale + bias_ref[...]
    row_max = jnp.max(logits, axis=1, keepdims=True)
    expo = jnp.exp(logits - row_max)
    total = jnp.sum(expo, axis=1, keepdims=True)
    probs = (expo / total).astype(bf16)
    o_latent = matmul(probs, win_ref[:, :LATENT]).astype(bf16)
    ol_ref[0] = o_latent
    oh_ref[...] = matmul(o_latent, w_ref[:, QN:]).astype(bf16)
    lse_ref[0] = jnp.broadcast_to(row_max + jnp.log(total), lse_ref.shape[1:])


def attend_back_kernel(
    scale,
    bh_ref,
    w_ref,
    win_ref,
    bias_ref,
    qf_ref,
    qn_ref,
    ol_ref,
    lse_ref,
    cos_ref,
    sin_ref,
    ge_ref,
    bqn_ref,
    rope_ref,
    own_ref,
    sib_ref,
    bwin_ref,
):
    head = pl.program_id(0)

    @pl.when(head == 0)
    def _():
        bwin_ref[...] = jnp.zeros_like(bwin_ref)
        rope_ref[...] = jnp.zeros_like(rope_ref)

    back_heads = bh_ref[...]
    ge_ref[:, QN:] = matmul_tn(ol_ref[0], back_heads).astype(bf16)
    back_olatent = matmul_nt(back_heads, w_ref[:, QN:]).astype(bf16)
    scores = matmul_nt(qf_ref[0], win_ref[...])
    probs = jnp.exp(scores * scale + bias_ref[...] - lse_ref[0][:, :1])
    back_probs = matmul_nt(back_olatent, win_ref[:, :LATENT])
    delta = jnp.sum(probs * back_probs, axis=1, keepdims=True)
    back_scores = (probs * (back_probs - delta) * scale).astype(bf16)
    bwin_ref[...] += matmul_tn(back_scores, qf_ref[0])
    bwin_ref[:, :LATENT] += matmul_tn(probs.astype(bf16), back_olatent)
    back_q = matmul(back_scores, win_ref[...])
    back_qlatent = back_q[:, :LATENT].astype(bf16)
    ge_ref[:, :QN] = matmul_tn(back_qlatent, qn_ref[...]).astype(bf16)
    bqn_ref[...] = matmul(back_qlatent, w_ref[:, :QN]).astype(bf16)
    halves = back_q[:, LATENT:]
    lane = lax.broadcasted_iota(jnp.int32, halves.shape, 1)
    crossed = jnp.where(lane < 32, pltpu.roll(halves, 96, 1), pltpu.roll(halves, 32, 1))
    turned = (halves * cos_ref[...] + crossed * sin_ref[...]).astype(bf16)
    rope_ref[...] += matmul_nt(turned, rope_places(head)).astype(bf16)

    @pl.when(head == pl.num_programs(0) - 1)
    def _():
        own_ref[...] = bwin_ref[: own_ref.shape[0]]
        sib_ref[...] = bwin_ref[own_ref.shape[0] :].astype(bf16)


def to_chip_order(values, core):
    lane = lax.broadcasted_iota(jnp.int32, (values.shape[0], 128), 1)
    low = (lane & 32) == 0
    sides = ([], [])
    for at in range(0, 1024, 128):
        first, second = values[:, at : at + 128], values[:, 1024 + at : 1152 + at]
        sides[0].append(jnp.where(low, first, pltpu.roll(second, 32, 1)))
        sides[1].append(jnp.where(low, pltpu.roll(first, 96, 1), second))
    side0, side1 = (jnp.concatenate(side, axis=1) for side in sides)
    mine = core == 0
    return jnp.where(mine, side0, side1), jnp.where(mine, side1, side0)


def from_chip_order(own, sibling, core):
    lane = lax.broadcasted_iota(jnp.int32, (own.shape[0], 128), 1)
    low = (lane & 32) == 0
    mine = core == 0
    side0, side1 = jnp.where(mine, own, sibling), jnp.where(mine, sibling, own)
    rows = ([], [])
    for at in range(0, 1024, 128):
        first, second = side0[:, at : at + 128], side1[:, at : at + 128]
        rows[0].append(jnp.where(low, first, pltpu.roll(second, 32, 1)))
        rows[1].append(jnp.where(low, pltpu.roll(first, 96, 1), second))
    return jnp.concatenate(rows[0] + rows[1], axis=1)


def enter_kernel(core_ref, x_ref, g_ref, x_out, inverse_out, g_out):
    values = x_ref[...].astype(f32)
    mean = jnp.mean(values * values, axis=1, keepdims=True)
    inverse_out[...] = jnp.broadcast_to(lax.rsqrt(mean + epsilon), inverse_out.shape)
    own, sibling = to_chip_order(values, core_ref[0])
    x_out[:, :1024] = own
    x_out[:, 1024:] = sibling
    own, sibling = to_chip_order(g_ref[...].astype(f32), core_ref[0])
    g_out[:, :1024] = own.astype(bf16)
    g_out[:, 1024:] = sibling.astype(bf16)


def dispatch_kernel(core_ref, mid_ref, gain_ref, pick_ref, h_ref, inverse_ref, rows_ref, true_ref):
    @pl.when(pl.program_id(0) == 0)
    def _():
        mid = mid_ref[...]
        inverse = lax.rsqrt(jnp.mean(mid * mid, axis=1, keepdims=True) + epsilon)
        inverse_ref[...] = jnp.broadcast_to(inverse, inverse_ref.shape)
        low = (mid * inverse * gain_ref[...]).astype(bf16)
        h_ref[...] = low
        wide = low.astype(f32)
        true_ref[...] = from_chip_order(wide[:, :1024], wide[:, 1024:], core_ref[0]).astype(bf16)

    rows_ref[...] = matmul(pick_ref[...], true_ref[...]).astype(bf16)


def combine_kernel(core_ref, pick_ref, rows_ref, base_ref, out_ref, total_ref):
    step = pl.program_id(0)

    @pl.when(step == 0)
    def _():
        total_ref[...] = jnp.zeros_like(total_ref)

    total_ref[...] += matmul_tn(pick_ref[...], rows_ref[...])

    @pl.when(step == pl.num_programs(0) - 1)
    def _():
        own, sibling = to_chip_order(total_ref[...], core_ref[0])
        out_ref[:, :1024] = (own + base_ref[:, :1024]).astype(bf16)
        out_ref[:, 1024:] = (sibling + base_ref[:, 1024:]).astype(bf16)


def routed_kernel(core_ref, weight_ref, rows_ref, base_ref, out_ref, total_ref):
    step = pl.program_id(0)

    @pl.when(step == 0)
    def _():
        total_ref[...] = from_chip_order(base_ref[:, :1024], base_ref[:, 1024:], core_ref[0])

    high, low = split_low(weight_ref[...])
    total_ref[...] += matmul_tn(high, rows_ref[...]) + matmul_tn(low, rows_ref[...])

    @pl.when(step == pl.num_programs(0) - 1)
    def _():
        out_ref[...] = total_ref[...].astype(bf16)


def leave_kernel(core_ref, mid_ref, part_ref, other_ref, out_ref):
    true = from_chip_order(mid_ref[:, :1024], mid_ref[:, 1024:], core_ref[0])
    out_ref[...] = (true + (part_ref[...].astype(f32) + other_ref[...].astype(f32))).astype(bf16)


def grad_kernel(core_ref, grad_ref, out_ref):
    out_ref[...] = from_chip_order(grad_ref[:, :1024], grad_ref[:, 1024:], core_ref[0])


def scalar_spec():
    return pl.BlockSpec(memory_space=pltpu.SMEM)


def local_kernel(body, name, grid, in_specs, out_specs, out_shape, scratch=(), flops=0, moved=4 << 20):
    return pl.pallas_call(
        body,
        grid=(grid,),
        in_specs=in_specs,
        out_specs=out_specs,
        out_shape=out_shape,
        scratch_shapes=scratch,
        compiler_params=pltpu.CompilerParams(vmem_limit_bytes=VMEM_BYTES),
        cost_estimate=pl.CostEstimate(flops=flops, bytes_accessed=moved, transcendentals=0),
        name=name,
    )


def whole(shape):
    return pl.BlockSpec(shape, lambda h: (0,) * len(shape))


def attend(scale, q_nope, rope, w_expand, window, bias):
    tok, heads, keys = q_nope.shape[0], q_nope.shape[1] // QN, window.shape[0]
    return pl.pallas_call(
        functools.partial(attend_kernel, scale),
        grid=(heads,),
        in_specs=[
            pl.BlockSpec((tok, QN), lambda h: (0, h)),
            whole((tok, 512)),
            pl.BlockSpec((LATENT, QN + DV), lambda h: (0, h)),
            whole((keys, WIDE)),
            whole((tok, keys)),
        ],
        out_specs=[
            pl.BlockSpec((1, tok, WIDE), lambda h: (h, 0, 0)),
            pl.BlockSpec((1, tok, LATENT), lambda h: (h, 0, 0)),
            pl.BlockSpec((tok, DV), lambda h: (0, h)),
            pl.BlockSpec((1, tok, 128), lambda h: (h, 0, 0)),
        ],
        out_shape=[
            jax.ShapeDtypeStruct((heads, tok, WIDE), bf16),
            jax.ShapeDtypeStruct((heads, tok, LATENT), bf16),
            jax.ShapeDtypeStruct((tok, heads * DV), bf16),
            jax.ShapeDtypeStruct((heads, tok, 128), f32),
        ],
        compiler_params=pltpu.CompilerParams(vmem_limit_bytes=VMEM_BYTES),
        cost_estimate=pl.CostEstimate(
            flops=heads * tok * keys * 2400, bytes_accessed=12 << 20, transcendentals=heads * tok * keys
        ),
        name="attend",
    )(q_nope, rope, w_expand, window, bias)


def attend_back(scale, back_heads, w_expand, window, bias, q_full, q_nope, o_latent, log_total, cos, sin):
    tok, heads, keys = q_nope.shape[0], q_nope.shape[1] // QN, window.shape[0]
    return pl.pallas_call(
        functools.partial(attend_back_kernel, scale),
        grid=(heads,),
        in_specs=[
            pl.BlockSpec((tok, DV), lambda h: (0, h)),
            pl.BlockSpec((LATENT, QN + DV), lambda h: (0, h)),
            whole((keys, WIDE)),
            whole((tok, keys)),
            pl.BlockSpec((1, tok, WIDE), lambda h: (h, 0, 0)),
            pl.BlockSpec((tok, QN), lambda h: (0, h)),
            pl.BlockSpec((1, tok, LATENT), lambda h: (h, 0, 0)),
            pl.BlockSpec((1, tok, 128), lambda h: (h, 0, 0)),
            whole((tok, 128)),
            whole((tok, 128)),
        ],
        out_specs=[
            pl.BlockSpec((LATENT, QN + DV), lambda h: (0, h)),
            pl.BlockSpec((tok, QN), lambda h: (0, h)),
            whole((tok, 512)),
            whole((5 * tok, WIDE)),
            whole((4 * tok, WIDE)),
        ],
        out_shape=[
            jax.ShapeDtypeStruct((LATENT, heads * (QN + DV)), bf16),
            jax.ShapeDtypeStruct((tok, heads * QN), bf16),
            jax.ShapeDtypeStruct((tok, 512), bf16),
            jax.ShapeDtypeStruct((5 * tok, WIDE), f32),
            jax.ShapeDtypeStruct((4 * tok, WIDE), bf16),
        ],
        scratch_shapes=[pltpu.VMEM((keys, WIDE), f32)],
        compiler_params=pltpu.CompilerParams(vmem_limit_bytes=VMEM_BYTES),
        cost_estimate=pl.CostEstimate(
            flops=heads * tok * keys * 6400, bytes_accessed=20 << 20, transcendentals=heads * tok * keys
        ),
        name="attend_back",
    )(back_heads, w_expand, window, bias, q_full, q_nope, o_latent, log_total, cos, sin)


def shards(
    hidden_in,
    prenorm,
    query_proj,
    latent_proj,
    midnorm,
    expand_proj,
    output_proj,
    postnorm,
    shared_gate,
    shared_up,
    shared_down,
    expert_gate,
    expert_up,
    expert_down,
    segments,
    routes,
    route_weights,
    cotangent,
):
    dp = lax.axis_index("dp")
    core = lax.axis_index("core")
    chip = lax.axis_index("y") * 4 + lax.axis_index("z")
    tok = hidden_in.shape[0]
    heads = query_proj.shape[1] // (QN + QR)
    half = D // 2
    expert_pos = chip * 2 + core
    score_scale = 1.0 / math.sqrt(QN + QR)

    y_pos = lax.axis_index("y")
    z_pos = lax.axis_index("z")
    y_low = y_pos < 2
    y_outer = (y_pos == 0) | (y_pos == 3)
    fs = shared_gate.shape[1]

    gains = jnp.stack([prenorm, postnorm, jnp.pad(midnorm, (0, 24))], axis=1)
    q_cols = query_proj.reshape(32, heads, QN + QR)
    l_cols = latent_proj[:, :LATENT].reshape(32, 2, 16, 2, 8).transpose(0, 3, 2, 1, 4)
    pack = jnp.concatenate(
        [
            q_cols[:, :, :QN].reshape(32, heads * QN),
            q_cols[:, :, QN : QN + 32].reshape(32, heads * 32),
            q_cols[:, :, QN + 32 :].reshape(32, heads * 32),
            l_cols.reshape(32, LATENT),
            latent_proj[:, LATENT:],
            jnp.pad(gains, ((0, 0), (0, 61))),
            output_proj.T,
            expand_proj.reshape(32, 512),
        ],
        axis=1,
    )
    pair = gather_dp(pack, dp)
    pack_c = jnp.concatenate([shared_gate, shared_up, shared_down.T], axis=1)

    place = jnp.arange(D, dtype=jnp.int32)
    place_l = jnp.arange(LATENT, dtype=jnp.int32)
    mid_at = ((place // 1024) ^ core) * 256 + (place // 32 % 32) * 8 + place % 32
    perm_m = ((mid_at[:, None] == place_l[None, :]) & (place % 32 < 8)[:, None]).astype(bf16)
    core_at = core.reshape(1)

    def near_low(values):
        low, high = values[:, :512], values[:, 512:]
        return jnp.where(y_low, low, high), jnp.where(y_low, high, low)

    def near_outer(values):
        ends = jnp.concatenate([values[:, :256], values[:, 768:]], axis=1)
        middle = values[:, 256:768]
        return jnp.where(y_outer, ends, middle), jnp.where(y_outer, middle, ends)

    def join_low(own, other):
        return jnp.concatenate(
            [jnp.where(y_low, own, other), jnp.where(y_low, other, own)], axis=1
        )

    def join_outer(own, other):
        ends = jnp.where(y_outer, own, other)
        middle = jnp.where(y_outer, other, own)
        return jnp.concatenate([ends[:, :256], middle, ends[:, 256:]], axis=1)

    cuts = (0, 1024, 2176, 3200)
    chip_rows = [pair[:, a:b].reshape(1, 1, 64, b - a) for a, b in zip(cuts, cuts[1:])]
    chip_rows.append(pair[:, 3200:].reshape(1, 1, 16, 2048))
    along_z, along_y = ("z", z_pos, 1), ("y", y_pos, 0)
    firsts = [along_z + (False,), along_z + (True,), along_y + (False,), along_y + (True,)]
    seconds = [along_y + (False,), along_y + (True,), along_z + (False,), along_z + (True,)]

    def pairs(blocks, got, axes):
        return [
            merged(own, other, pos >= 2 if cross else pos % 2 == 1, dim)
            for own, other, (_, pos, dim, cross) in zip(blocks, got, axes)
        ]

    pair_c = gather_dp(pack_c, dp)
    blocks, got, pair_c, core_at, hidden_in, cotangent, routes, segments, y_late, z_late = together(
        chip_rows, gather_step(chip_rows, firsts, False), pair_c, core_at, hidden_in, cotangent,
        routes, segments, y_pos, z_pos,
    )
    blocks = pairs(blocks, got, firsts)
    blocks, got = together(blocks, gather_step(blocks, firsts, True))
    blocks = [joined(o, g, p, c, d) for o, g, (_, p, d, c) in zip(blocks, got, firsts)]
    blocks, got = together(blocks, gather_step(blocks, seconds, False))
    blocks = pairs(blocks, got, seconds)
    got = gather_step(blocks, seconds, True)
    near_sib = [swapped(block, "core") for block in blocks[:2]]

    inputs, inverse_one, up_low = local_kernel(
        enter_kernel,
        "enter",
        1,
        [scalar_spec(), whole((tok, D)), whole((tok, D))],
        [whole((tok, D)), whole((tok, 128)), whole((tok, D))],
        [
            jax.ShapeDtypeStruct((tok, D), f32),
            jax.ShapeDtypeStruct((tok, 128), f32),
            jax.ShapeDtypeStruct((tok, D), bf16),
        ],
    )(core_at, hidden_in, cotangent)
    inverse_one = inverse_one[:, :1]

    expert_ids = jnp.arange(32, dtype=jnp.int32)
    hits = routes[:, :, None] == expert_ids[None, None, :]
    named = jnp.sum(hits.astype(f32), axis=1)
    weight_te = jnp.sum(jnp.where(hits, route_weights[:, :, None], 0.0), axis=1)
    order = jnp.arange(tok, dtype=jnp.int32)
    earlier = (order[:, None] > order[None, :]).astype(bf16)
    rank = matmul(earlier, named.astype(bf16))
    rank_et = jnp.where(named > 0.5, rank, -1.0).T
    slot_ids = jnp.arange(SLOTS, dtype=jnp.int32).astype(f32)
    taken = rank_et[:, None, :] == slot_ids[None, :, None]
    slot_pick = taken.astype(bf16).reshape(32 * SLOTS, tok)
    slot_weight = jnp.where(taken, weight_te.T[:, None, :], 0.0).reshape(32 * SLOTS, tok)
    slot_pick, slot_weight = together(slot_pick, slot_weight)
    weight_hi, weight_lo = split_low(slot_weight)

    def exchange(rows):
        blocks = rows.reshape(32, SLOTS, rows.shape[1])
        return lax.all_to_all(blocks, EXPERT, split_axis=0, concat_axis=0, tiled=True).reshape(
            rows.shape
        )

    second = lax.axis_index("tensor") == 1
    grad_cols = jnp.where(second, cotangent[:, half:], cotangent[:, :half])
    grad_send = (matmul(weight_hi, grad_cols) + matmul(weight_lo, grad_cols)).astype(bf16)
    places = [
        stream_places(half, first, cross, y_late, z_late)
        for first, cross in (("z", False), ("z", True), ("y", False))
    ]
    x_places = stream_places(256, "y", True, y_late, z_late)

    block_chip = jnp.concatenate(
        [chip - 4 + jnp.arange(5, dtype=jnp.int32), chip - 4 + core + jnp.arange(4, dtype=jnp.int32)]
    )
    block_core = jnp.concatenate(
        [jnp.full((5,), core, jnp.int32), jnp.full((4,), 1 - core, jnp.int32)]
    )
    block_id = block_chip * 2 + block_core
    seg_blocks = lax.dynamic_slice_in_dim(segments.reshape(2, 32, tok), dp, 1, 0)[0]
    chosen = jnp.arange(32, dtype=jnp.int32)[None, :, None] == block_id[:, None, None]
    seg_keys = jnp.sum(jnp.where(chosen, seg_blocks[None] + 1, 0), axis=1).reshape(9 * tok) - 1
    seg_query = lax.dynamic_index_in_dim(seg_blocks, expert_pos, 0, keepdims=False)
    key_pos = (block_id[:, None] * tok + jnp.arange(tok, dtype=jnp.int32)[None, :]).reshape(9 * tok)
    query_pos = expert_pos * tok + jnp.arange(tok, dtype=jnp.int32)
    offsets = query_pos[:, None] - key_pos[None, :]
    visible = (seg_query[:, None] == seg_keys[None, :]) & (offsets >= 0) & (offsets < WIN)

    bias = jnp.where(visible, 0.0, neg_big)
    positions = (expert_pos * tok + jnp.arange(tok, dtype=jnp.int32)).astype(f32)
    cosine, sine_tab = rope_tables(positions, QR)
    cos_all = jnp.tile(cosine, (1, heads))
    sin_all = jnp.tile(sine_tab, (1, heads))

    (
        blocks, got, inputs, inverse_one, up_low, slot_pick, slot_weight, grad_send, pair_c, bias,
        cosine, sine_tab, cos_all, sin_all, perm_m, places, x_places,
    ) = together(
        blocks, got, inputs, inverse_one, up_low, slot_pick, slot_weight, grad_send, pair_c, bias,
        cosine, sine_tab, cos_all, sin_all, perm_m, places, x_places,
    )
    grad_half = exchange(grad_send)
    upstream = up_low.astype(f32)
    q_parts = [
        w.reshape(512, 1024) for w in (blocks[0], got[0], near_sib[0], swapped(got[0], "core"))
    ]
    l_parts = [
        w.reshape(512, 1152) for w in (blocks[1], got[1], near_sib[1], swapped(got[1], "core"))
    ]
    own_c = lax.all_gather(pair_c, PLANE, axis=0, tiled=True)
    up_pair = both_cores(up_low[:, :half], swapped(up_low[:, half:], "core"))

    pick = jnp.eye(8, 64, dtype=bf16)
    gain_parts = [matmul_nt(pick, w[:, 1088:]) for w in l_parts]
    gain_rows = jnp.concatenate(
        [join_outer(gain_parts[0], gain_parts[1]), join_outer(gain_parts[2], gain_parts[3])], axis=1
    )
    gain_one = gain_rows[0]
    gain_two = gain_rows[1]
    gain_mid = matmul(gain_rows.astype(bf16), perm_m)[2]

    h_one = (inputs * inverse_one * gain_one).astype(bf16)
    h_parts = near_outer(h_one[:, :half]) + near_outer(h_one[:, half:])
    kv_all = sum(matmul(h, w) for h, w in zip(h_parts, l_parts))
    h_parts = near_low(h_one[:, :half]) + near_low(h_one[:, half:])
    q_nope = sum(matmul(h, w) for h, w in zip(h_parts, q_parts)).astype(bf16)
    q_first = kv_all[:, :256]
    q_second = kv_all[:, 256:512]
    kv_pre = kv_all[:, 512:1088]
    latent_raw = kv_pre[:, :LATENT]
    latent_normed, inverse_mid = rms_forward(latent_raw, gain_mid)
    latent = jnp.concatenate(
        [
            latent_normed,
            rotate(kv_pre[:, LATENT:], cosine, sine_tab),
            jnp.zeros((tok, WIDE - LATENT - QR), f32),
        ],
        axis=1,
    ).astype(bf16)
    latent, blocks, got = together(latent, blocks[2:], got[2:])
    w_out_own = joined(blocks[0], got[0], z_pos, False, 1).reshape(half, heads * DV)
    w_out_sib = swapped(w_out_own, "core")
    x_own = joined(blocks[1], got[1], z_pos, True, 1).reshape(256, heads * (QN + DV))
    x_sib = swapped(x_own, "core")
    w_expand = jnp.concatenate(
        [jnp.where(core == 0, x_own, x_sib), jnp.where(core == 0, x_sib, x_own)], axis=0
    )
    rope = jnp.concatenate(
        [q_first * cos_all - q_second * sin_all, q_first * sin_all + q_second * cos_all], axis=1
    ).astype(bf16)
    shifts = [chip_shift(latent, k) for k in (4, 3, 2, 1)]
    shifts, latent, q_nope, rope, w_expand = together(shifts, latent, q_nope, rope, w_expand)
    own_blocks = jnp.stack(shifts + [latent])
    sib_blocks = swapped(
        lax.dynamic_slice_in_dim(own_blocks, 1 - core, 4, 0), "core"
    )
    window = jnp.concatenate([own_blocks, sib_blocks], axis=0).reshape(9 * tok, WIDE)
    window, grad_half = together(window, grad_half)
    q_full, o_latent, o_heads, log_total = attend(
        score_scale, q_nope, rope, w_expand, window, bias
    )
    o_part = jnp.concatenate(
        [matmul_nt(o_heads, w_out_own), matmul_nt(o_heads, w_out_sib)], axis=1
    ).astype(bf16)
    o_part = lax.optimization_barrier(o_part)
    mid = inputs + (o_part.astype(f32) + swapped(o_part, "tensor").astype(f32))
    h_one_pair = both_cores(h_one[:, :half], swapped(h_one[:, half:], "core"))
    h_orders = [matmul(h_one_pair, p).astype(bf16) for p in places]
    mid, grad_half, h_orders = together(mid, grad_half, h_orders)
    grad_other = swapped(grad_half, "tensor")

    slots = 32 * SLOTS
    h_two, inverse_two, send_rows = local_kernel(
        dispatch_kernel,
        "dispatch",
        4,
        [
            scalar_spec(),
            whole((tok, D)),
            whole((1, D)),
            pl.BlockSpec((slots // 4, tok), lambda i: (i, 0)),
        ],
        [
            whole((tok, D)),
            whole((tok, 128)),
            pl.BlockSpec((slots // 4, D), lambda i: (i, 0)),
        ],
        [
            jax.ShapeDtypeStruct((tok, D), bf16),
            jax.ShapeDtypeStruct((tok, 128), f32),
            jax.ShapeDtypeStruct((slots, D), bf16),
        ],
        [pltpu.VMEM((tok, D), bf16)],
        flops=2 * slots * tok * D,
        moved=6 << 20,
    )(core_at, mid, gain_two[None, :], slot_pick)
    inverse_two = inverse_two[:, :1]
    expert_rows = exchange(send_rows)

    h_two_pair = both_cores(h_two[:, :half], swapped(h_two[:, half:], "core"))
    s_all = jnp.concatenate(
        [matmul(h_two_pair, own_c[:, : 2 * fs]), matmul(up_pair, own_c[:, 2 * fs :])], axis=1
    )
    s_mine = s_all[:tok] + swapped(s_all[tok:].astype(bf16), "core").astype(f32)
    s_gate = s_mine[:, :fs]
    s_up = s_mine[:, fs : 2 * fs]
    back_shidden = s_mine[:, 2 * fs :]
    s_sig = jax.nn.sigmoid(s_gate)
    s_active = s_gate * s_sig
    s_hidden = (s_active * s_up).astype(bf16)
    back_sgate = (back_shidden * s_up * s_sig * (1.0 + s_gate * (1.0 - s_sig))).astype(bf16)
    back_sup = (back_shidden * s_active).astype(bf16)
    s_acts = jnp.concatenate([back_sgate, back_sup, s_hidden], axis=1)
    s_pair = both_cores(s_acts, swapped(s_acts, "core"))
    shared_rows = jnp.concatenate(
        [matmul_tn(h_two_pair, s_pair[:, : 2 * fs]), matmul_tn(up_pair, s_pair[:, 2 * fs :])], axis=1
    ).astype(bf16)
    grad_rows = jnp.concatenate(
        [jnp.where(second, grad_other, grad_half), jnp.where(second, grad_half, grad_other)], axis=1
    )
    expert_rows, s_pair, shared_rows, grad_rows = together(
        expert_rows, s_pair, shared_rows, grad_rows
    )
    shared_part = lax.psum_scatter(shared_rows, PLANE, scatter_dimension=0, tiled=True)
    wide_all = jnp.concatenate(
        [
            matmul_nt(s_pair[:, : 2 * fs], own_c[:, : 2 * fs]),
            matmul_nt(s_pair[:, 2 * fs :], own_c[:, 2 * fs :]),
        ],
        axis=1,
    )
    wide_got = swapped(wide_all[tok:].astype(bf16), "core").astype(f32)
    shared_back = jnp.concatenate([wide_all[:tok, :half], wide_got[:, :half]], axis=1)
    s_part = jnp.concatenate([wide_all[:tok, half:], wide_got[:, half:]], axis=1)
    gate_pre = matmul(expert_rows, expert_gate[0])
    up_pre = matmul(expert_rows, expert_up[0])
    gate_sig = jax.nn.sigmoid(gate_pre)
    active = gate_pre * gate_sig
    hidden = (active * up_pre).astype(bf16)
    back_hidden = matmul_nt(grad_rows, expert_down[0])
    back_gate = (back_hidden * up_pre * gate_sig * (1.0 + gate_pre * (1.0 - gate_sig))).astype(bf16)
    back_up = (back_hidden * active).astype(bf16)
    row_grad = (matmul_nt(back_gate, expert_gate[0]) + matmul_nt(back_up, expert_up[0])).astype(bf16)
    row_back = exchange(row_grad)
    e_part = matmul(hidden, expert_down[0]).astype(bf16)
    gate_low = [
        matmul_tn(expert_rows[:, :half], back_gate).astype(bf16),
        matmul_tn(expert_rows[:, half:], back_gate).astype(bf16),
    ]
    up_low_grad = [
        matmul_tn(expert_rows[:, :half], back_up).astype(bf16),
        matmul_tn(expert_rows[:, half:], back_up).astype(bf16),
    ]
    down_low = [
        matmul_tn(hidden, grad_rows[:, :1536]).astype(bf16),
        matmul_tn(hidden, grad_rows[:, 1536:]).astype(bf16),
    ]
    down_got = swapped(down_low[0], "dp")
    row_back, down_got, gate_low, up_low_grad, e_part, s_part, shared_back = together(
        row_back, down_got, gate_low, up_low_grad, e_part, s_part, shared_back
    )
    returned = exchange(e_part)
    back_part = local_kernel(
        combine_kernel,
        "combine",
        4,
        [
            scalar_spec(),
            pl.BlockSpec((slots // 4, tok), lambda i: (i, 0)),
            pl.BlockSpec((slots // 4, D), lambda i: (i, 0)),
            whole((tok, D)),
        ],
        whole((tok, D)),
        jax.ShapeDtypeStruct((tok, D), bf16),
        [pltpu.VMEM((tok, D), f32)],
        flops=2 * slots * tok * D,
        moved=6 << 20,
    )(core_at, slot_pick, row_back, shared_back)
    back_two = back_part.astype(f32) + swapped(back_part, "tensor").astype(f32)
    back_midnorm, grad_gain_two = rms_backward(mid, inverse_two, gain_two, back_two)
    back_mid = upstream + back_midnorm
    back_attn = back_mid.astype(bf16)
    back_attn, grad_gain_two, back_mid, gate_low, up_low_grad, down_low = together(
        back_attn, grad_gain_two, back_mid, gate_low, up_low_grad, down_low
    )
    down_got = [down_got, swapped(down_low[1], "dp")]
    gate_got = [swapped(part, "dp") for part in gate_low]
    up_got = [swapped(part, "dp") for part in up_low_grad]

    attn_pair = both_cores(back_attn[:, :half], swapped(back_attn[:, half:], "core"))
    attn_orders = [matmul(attn_pair, p).astype(bf16) for p in places[1:]]
    heads_pair = both_cores(o_heads, swapped(o_heads, "core"))
    gain_low = grad_gain_two.astype(bf16)
    gain_sum = add_low(gain_low[:half], swapped(gain_low[half:], "core"))
    gain_col = matmul_tn(places[2], jnp.broadcast_to(gain_sum[:, None], (half, 128))).astype(bf16)

    back_heads = (
        matmul(back_attn[:, :half], w_out_own) + matmul(back_attn[:, half:], w_out_sib)
    ).astype(bf16)
    pad_lanes = jnp.zeros((tok, 64), f32)
    grad_expand, back_qnope, back_rope, back_own, back_sib = attend_back(
        score_scale,
        back_heads,
        w_expand,
        window,
        bias,
        q_full,
        q_nope,
        o_latent,
        log_total,
        jnp.concatenate([cosine, cosine, pad_lanes], axis=1),
        jnp.concatenate([sine_tab, -sine_tab, pad_lanes], axis=1),
    )
    back_qnope, back_rope, back_own, back_sib, grad_expand, down_got[1] = together(
        back_qnope, back_rope, back_own, back_sib, grad_expand, down_got[1]
    )
    acts_q = jnp.concatenate([back_qnope, back_rope], axis=1)
    expand_mine = lax.dynamic_slice_in_dim(grad_expand, core * 256, 256, 0)
    expand_theirs = lax.dynamic_slice_in_dim(grad_expand, 256 - core * 256, 256, 0)
    from_sib, acts_other, expand_other, acts_q, expand_mine, heads_pair, attn_orders, down_low = together(
        swapped(back_sib, "core"),
        swapped(acts_q, "core"),
        swapped(expand_theirs, "core"),
        acts_q,
        expand_mine,
        heads_pair,
        attn_orders,
        down_low,
    )

    from_sib = from_sib.astype(f32).reshape(4, tok, WIDE)
    pad_block = jnp.zeros((1, tok, WIDE), f32)
    from_sib = jnp.where(
        core == 0,
        jnp.concatenate([pad_block, from_sib], axis=0),
        jnp.concatenate([from_sib, pad_block], axis=0),
    )
    chip_blocks = back_own.reshape(5, tok, WIDE) + from_sib
    shifts = [chip_shift(chip_blocks[4 - k].astype(bf16), -k) for k in (4, 3, 2, 1)]

    acts_q = both_cores(acts_q, acts_other)
    rows_x = add_low(expand_mine, expand_other)
    rows_x = matmul_tn(x_places, rows_x).astype(bf16).reshape(4, 4, 64, 512)

    def halves(part):
        at = slice(0, 512) if part == 0 else slice(512, 1024)
        q_first = matmul_tn(h_orders[0][:, at], acts_q[:, :896])
        q_second = jnp.concatenate(
            [
                matmul_tn(h_orders[1][:, at], acts_q[:, 896:]),
                matmul_tn(attn_orders[0][:, at], heads_pair[:, :256]),
            ],
            axis=1,
        )
        third = jnp.concatenate(
            [matmul_tn(attn_orders[1][:, at], heads_pair[:, 256:]).astype(bf16), gain_col[at]], axis=1
        )
        rows = [r.astype(bf16).reshape(2, 4, 64, 896) for r in (q_first, q_second, third)]
        return rows + [rows_x[2 * part : 2 * part + 2]]

    first_steps = [steps_of("z", False), steps_of("z", True), steps_of("y", False), steps_of("y", True)]
    down_sum = summed(down_low, down_got, 1)
    sends = halves(0)
    (
        sends, rows_x, chip_last, shifts, gate_got[0], h_orders, attn_orders, down_sum, shared_part,
    ) = together(
        sends, rows_x, chip_blocks[4], shifts, gate_got[0], h_orders, attn_orders, down_sum,
        shared_part,
    )
    got = [xored(r, *steps[0]) for r, steps in zip(sends, first_steps)]
    keeps = halves(1)

    back_latent = chip_last + sum(shift.astype(f32) for shift in shifts)

    back_raw, grad_gain_mid = rms_backward(
        latent_raw, inverse_mid, gain_mid, back_latent[:, :LATENT]
    )
    back_kvpre = jnp.concatenate(
        [back_raw, rotate(back_latent[:, LATENT : LATENT + QR], cosine, -sine_tab)], axis=1
    ).astype(bf16)
    kv_pair = both_cores(back_kvpre, swapped(back_kvpre, "core"))
    mid_low = grad_gain_mid.astype(bf16)
    mid_sum = (mid_low.astype(f32) + swapped(mid_low, "core").astype(f32)).astype(bf16)
    mid_col = matmul_nt(perm_m[:half], jnp.broadcast_to(mid_sum[None, :], (64, LATENT)))
    mid_col = matmul_tn(places[2], mid_col.astype(bf16))
    rows_l = jnp.concatenate([matmul_tn(h_orders[2], kv_pair), mid_col], axis=1)
    rows_l = rows_l.astype(bf16).reshape(4, 4, 64, 640)

    got, keeps, rows_l, gate_got[1], back_mid, returned, gate_low, up_low_grad = together(
        got, keeps, rows_l, gate_got[1], back_mid, returned, gate_low, up_low_grad
    )
    out_low = local_kernel(
        routed_kernel,
        "routed",
        4,
        [
            scalar_spec(),
            pl.BlockSpec((slots // 4, tok), lambda i: (i, 0)),
            pl.BlockSpec((slots // 4, D), lambda i: (i, 0)),
            whole((tok, D)),
        ],
        whole((tok, D)),
        jax.ShapeDtypeStruct((tok, D), bf16),
        [pltpu.VMEM((tok, D), f32)],
        flops=4 * slots * tok * D,
        moved=6 << 20,
    )(core_at, slot_weight, returned, s_part)
    near = [add_low(k[0], g[0]) for k, g in zip(keeps, got)]
    far = [add_low(k[1], g[1]) for k, g in zip(keeps, got)]

    got = [xored(r, *steps[1]) for r, steps in zip(far, first_steps)]
    got_l = xored(rows_l[:2], "y", 1)
    got, near, got_l, rows_l, out_low, gate_low, back_qnope, back_rope, back_kvpre, up_got[0] = together(
        got, near, got_l, rows_l, out_low, gate_low, back_qnope, back_rope, back_kvpre, up_got[0]
    )
    back_lane = jnp.concatenate([back_rope, back_kvpre, jnp.zeros((tok, 64), bf16)], axis=1)
    q_back = [matmul_nt(back_qnope, w) for w in q_parts]
    l_back = [matmul_nt(back_lane, w) for w in l_parts]
    one_part = jnp.concatenate(
        [
            join_low(q_back[0], q_back[1]) + join_outer(l_back[0], l_back[1]),
            join_low(q_back[2], q_back[3]) + join_outer(l_back[2], l_back[3]),
        ],
        axis=1,
    ).astype(bf16)

    one_other = swapped(one_part, "tensor")
    out_other = swapped(out_low, "tensor")
    gate_sum = summed(gate_low, gate_got, 0)
    rows = [add_low(n, g) for n, g in zip(near, got)]
    near_l, far_l = add_low(rows_l[2], got_l[0]), add_low(rows_l[3], got_l[1])
    got_l = xored(far_l, "y", 3)

    def owned(blocks, axis):
        blocks = blocks.reshape(8, 32, blocks.shape[2])
        blocks = lax.all_to_all(blocks, (axis, "dp"), split_axis=0, concat_axis=0, tiled=True)
        return jnp.sum(blocks.astype(f32), axis=0)

    from_y = owned(jnp.concatenate(rows[:2], axis=2), "y")
    got_l, near_l, rows, from_y, gate_sum, shared_part, one_part, out_other, out_low, up_got[1] = together(
        got_l, near_l, rows, from_y, gate_sum, shared_part, one_part, out_other, out_low, up_got[1]
    )
    from_z = owned(jnp.concatenate(rows[2:] + [add_low(near_l, got_l)], axis=2), "z")
    l_sum = from_z[:, 1408:]


    got = [xored(r, *steps[1]) for r, steps in zip(far, first_steps)]
    got_l = xored(rows_l[:2], "y", 1)
    got, near, got_l, rows_l, out_low, gate_low, back_qnope, back_rope, back_kvpre, up_got[0] = together(
        got, near, got_l, rows_l, out_low, gate_low, back_qnope, back_rope, back_kvpre, up_got[0]
    )
    back_lane = jnp.concatenate([back_rope, back_kvpre, jnp.zeros((tok, 64), bf16)], axis=1)
    q_back = [matmul_nt(back_qnope, w) for w in q_parts]
    l_back = [matmul_nt(back_lane, w) for w in l_parts]
    one_part = jnp.concatenate(
        [
            join_low(q_back[0], q_back[1]) + join_outer(l_back[0], l_back[1]),
            join_low(q_back[2], q_back[3]) + join_outer(l_back[2], l_back[3]),
        ],
        axis=1,
    ).astype(bf16)

    one_other = swapped(one_part, "tensor")
    out_other = swapped(out_low, "tensor")
    gate_sum = summed(gate_low, gate_got, 0)
    rows = [add_low(n, g) for n, g in zip(near, got)]
    near_l, far_l = add_low(rows_l[2], got_l[0]), add_low(rows_l[3], got_l[1])
    got_l = xored(far_l, "y", 3)

    def owned(blocks, axis):
        blocks = blocks.reshape(8, 32, blocks.shape[2])
        blocks = lax.all_to_all(blocks, (axis, "dp"), split_axis=0, concat_axis=0, tiled=True)
        return jnp.sum(blocks.astype(f32), axis=0)

    from_y = owned(jnp.concatenate(rows[:2], axis=2), "y")
    got_l, near_l, rows, from_y, gate_sum, shared_part, one_part, out_other, out_low, up_got[1] = together(
        got_l, near_l, rows, from_y, gate_sum, shared_part, one_part, out_other, out_low, up_got[1]
    )
    from_z = owned(jnp.concatenate(rows[2:] + [add_low(near_l, got_l)], axis=2), "z")
    l_sum = from_z[:, 1408:]

    back_one = one_part.astype(f32) + one_other.astype(f32)
    back_innorm, _ = rms_backward(inputs, inverse_one, gain_one, back_one)
    input_grad = local_kernel(
        grad_kernel,
        "input_order",
        1,
        [scalar_spec(), whole((tok, D))],
        whole((tok, D)),
        jax.ShapeDtypeStruct((tok, D), f32),
    )(core_at, back_mid + back_innorm)

    output = local_kernel(
        leave_kernel,
        "leave",
        1,
        [scalar_spec()] + [whole((tok, D))] * 3,
        whole((tok, D)),
        jax.ShapeDtypeStruct((tok, D), bf16),
    )(core_at, mid, out_low, out_other)

    shared_grads = finish_rows(shared_part, dp)
    out_grads = jnp.concatenate([from_y[:, 1536:], from_z[:, :768]], axis=1)
    weight_dots = jnp.sum(from_y[:, :1536] * pack[:, :1536].astype(f32), axis=1) + jnp.sum(
        l_sum[:, :576] * pack[:, 1536:2112].astype(f32), axis=1
    )
    small = jnp.concatenate(
        [
            l_sum,
            (weight_dots / prenorm.astype(f32))[:, None],
            0.5 * from_z[:, 768:769],
            jnp.zeros((32, 126), f32),
        ],
        axis=1,
    )
    small = small + swapped(small, "tensor")
    query_grad = jnp.concatenate(
        [
            from_y[:, :1024].reshape(32, heads, QN),
            from_y[:, 1024:1280].reshape(32, heads, 32),
            from_y[:, 1280:1536].reshape(32, heads, 32),
        ],
        axis=2,
    ).reshape(32, heads * (QN + QR))
    latent_cols = small[:, :LATENT].reshape(32, 2, 16, 2, 8).transpose(0, 3, 2, 1, 4)
    latent_grad = jnp.concatenate(
        [latent_cols.reshape(32, LATENT), small[:, LATENT : LATENT + QR]], axis=1
    )

    return (
        output,
        input_grad,
        small[:, 640],
        query_grad,
        latent_grad,
        small[:8, 576],
        from_z[:, 896:1408].reshape(8, 2048),
        out_grads.T,
        small[:, 641],
        shared_grads[:, :fs],
        shared_grads[:, fs : 2 * fs],
        shared_grads[:, 2 * fs :].T,
        gate_sum[None],
        summed(up_low_grad, up_got, 0)[None],
        down_sum[None],
    )


def solution(mesh):
    fine = Mesh(
        mesh.devices.reshape(2, 4, 4, 2, 2), ("dp", "y", "z", "core", "tensor")
    )
    rows = ("dp", "y", "z", "core")
    placed = (
        P(rows, None),
        P(rows),
        P(rows, "tensor"),
        P(rows, None),
        P(rows),
        P(rows, "tensor"),
        P("tensor", rows),
        P(rows),
        P(rows, "tensor"),
        P(rows, "tensor"),
        P("tensor", rows),
        P(EXPERT, None, "tensor"),
        P(EXPERT, None, "tensor"),
        P(EXPERT, "tensor", None),
        P(),
        P(rows, None),
        P(rows, None),
        P(rows, None),
    )
    return jax.shard_map(
        shards,
        mesh=fine,
        in_specs=placed,
        out_specs=(
            P(rows, None),
            P(rows, None),
            P(rows),
            P(rows, "tensor"),
            P(rows, None),
            P(rows),
            P(rows, "tensor"),
            P("tensor", rows),
            P(rows),
            P(rows, "tensor"),
            P(rows, "tensor"),
            P("tensor", rows),
            P(EXPERT, None, "tensor"),
            P(EXPERT, None, "tensor"),
            P(EXPERT, "tensor", None),
        ),
        check_vma=False,
    )
```

```python
import functools
import math

import jax
import jax.numpy as jnp
from jax import lax
from jax.experimental import pallas as pl
from jax.experimental.pallas import tpu as pltpu
from jax.sharding import Mesh, PartitionSpec as P

D = 2048
QN = 128
QR = 64
DV = 128
LATENT = 512
TOPK = 6
WIN = 1024
SLOTS = 32

epsilon = 1e-06
neg_big = -1e30
f32 = jnp.float32
bf16 = jnp.bfloat16
PLANE = ("y", "z")
EXPERT = ("y", "z", "core")


def swapped(block, axis):
    return lax.ppermute(block, axis, [(0, 1), (1, 0)])


def chip_shift(block, distance):
    chips = range(16)
    route = [(i - distance, i) for i in chips if i - distance in chips]
    return lax.ppermute(block, PLANE, route)


def core_shift(block, first, second):
    route = [
        (2 * i + c, 2 * (i + k) + c) for c, k in ((0, first), (1, second)) for i in range(16 - k)
    ]
    return lax.ppermute(block, EXPERT, route)


def matmul(left_op, right_op):
    return jnp.dot(left_op, right_op, preferred_element_type=f32)


def matmul_tn(left_op, right_op):
    return lax.dot_general(
        left_op, right_op, (((0,), (0,)), ((), ())), preferred_element_type=f32
    )


def matmul_nt(left_op, right_op):
    return lax.dot_general(
        left_op, right_op, (((1,), (1,)), ((), ())), preferred_element_type=f32
    )


def pair_sum(part, axis):
    low = lax.optimization_barrier(part.astype(bf16))
    return low.astype(f32) + swapped(low, axis).astype(f32)


def split_low(values):
    high = values.astype(bf16)
    return high, (values - high.astype(f32)).astype(bf16)


def rms_forward(values, gain_vec):
    inverse = lax.rsqrt(jnp.mean(values * values, axis=-1, keepdims=True) + epsilon)
    return (values * inverse * gain_vec, inverse)


def rms_backward(values, inverse, gain_vec, upstream):
    scaled = upstream * gain_vec
    inner_mean = jnp.mean(scaled * values, axis=-1, keepdims=True)
    back_values = inverse * (scaled - values * inner_mean * inverse * inverse)
    gain_grad = jnp.sum(upstream * values * inverse, axis=0)
    return (back_values, gain_grad)


def rope_tables(positions, width):
    half_width = width // 2
    frequency = jnp.exp(
        -math.log(10000.0) * jnp.arange(half_width, dtype=f32) * (2.0 / width)
    )
    angles = positions[:, None] * frequency[None, :]
    return (jnp.cos(angles), jnp.sin(angles))


def rotate(values, cosine, sine_tab):
    half_width = values.shape[-1] // 2
    first_half = values[..., :half_width]
    second_half = values[..., half_width:]
    return jnp.concatenate(
        [
            first_half * cosine - second_half * sine_tab,
            first_half * sine_tab + second_half * cosine,
        ],
        axis=-1,
    )


def xored(block, axis, k):
    return lax.ppermute(block, axis, [(i, i ^ k) for i in range(4)])


def merged(own, other, upper, dim):
    return jnp.concatenate(
        [jnp.where(upper, other, own), jnp.where(upper, own, other)], axis=dim
    )


def joined(own, other, pos, cross, dim):
    if not cross:
        return merged(own, other, pos >= 2, dim)
    outer = (pos == 0) | (pos == 3)
    ends = jnp.where(outer, own, other)
    middle = jnp.where(outer, other, own)
    low, high = jnp.split(ends, 2, axis=dim)
    return jnp.concatenate([low, middle, high], axis=dim)


def together(*trees):
    return lax.optimization_barrier(trees)


def gather_step(blocks, axes, second):
    return [
        xored(block, axis, 1 if cross == second else 3)
        for block, (axis, _, _, cross) in zip(blocks, axes)
    ]


def summed(mine, other, dim):
    return jnp.concatenate(mine, axis=dim).astype(f32) + jnp.concatenate(other, axis=dim).astype(f32)


def add_low(left, right):
    return (left.astype(f32) + right.astype(f32)).astype(bf16)


def gather_dp(pack, dp):
    other = swapped(pack, "dp")
    return jnp.concatenate(
        [jnp.where(dp == 0, pack, other), jnp.where(dp == 0, other, pack)], axis=0
    )


def mine_of(part, dp):
    return lax.dynamic_index_in_dim(part, dp, 0, keepdims=False)


def theirs_of(part, dp):
    return lax.dynamic_index_in_dim(part, 1 - dp, 0, keepdims=False)


def finish_rows(part, dp):
    part = part.reshape(2, 32, part.shape[1])
    mine = lax.dynamic_index_in_dim(part, dp, 0, keepdims=False)
    theirs = lax.dynamic_index_in_dim(part, 1 - dp, 0, keepdims=False)
    return mine.astype(f32) + swapped(theirs, "dp").astype(f32)


def both_cores(own, sibling):
    return jnp.concatenate([own, sibling], axis=0)


WIDE = 640
VMEM_BYTES = 56 * 1024 * 1024


def rope_places(head):
    row = lax.broadcasted_iota(jnp.int32, (512, 128), 0)
    lane = lax.broadcasted_iota(jnp.int32, (512, 128), 1)
    wanted = lax.shift_right_logical(lane, 5) * 256 + head * 32 + (lane & 31)
    return jnp.where((lane < 64) & (row == wanted), 1.0, 0.0).astype(bf16)


def attend_kernel(scale, qn_ref, rope_ref, w_ref, win_ref, bias_ref, qf_ref, ol_ref, oh_ref, lse_ref):
    q_latent = matmul_nt(qn_ref[...], w_ref[:, :QN]).astype(bf16)
    q_rope = matmul(rope_ref[...], rope_places(pl.program_id(0))).astype(bf16)
    qf_ref[0, :, :LATENT] = q_latent
    qf_ref[0, :, LATENT:] = q_rope
    scores = matmul_nt(q_latent, win_ref[:, :LATENT]) + matmul_nt(q_rope, win_ref[:, LATENT:])
    logits = scores * scale + bias_ref[...]
    row_max = jnp.max(logits, axis=1, keepdims=True)
    expo = jnp.exp(logits - row_max)
    total = jnp.sum(expo, axis=1, keepdims=True)
    probs = (expo / total).astype(bf16)
    o_latent = matmul(probs, win_ref[:, :LATENT]).astype(bf16)
    ol_ref[0] = o_latent
    oh_ref[...] = matmul(o_latent, w_ref[:, QN:]).astype(bf16)
    lse_ref[0] = jnp.broadcast_to(row_max + jnp.log(total), lse_ref.shape[1:])


def attend_back_kernel(
    scale,
    bh_ref,
    w_ref,
    win_ref,
    bias_ref,
    qf_ref,
    qn_ref,
    ol_ref,
    lse_ref,
    cos_ref,
    sin_ref,
    ge_ref,
    bqn_ref,
    rope_ref,
    own_ref,
    sib_ref,
    bwin_ref,
):
    head = pl.program_id(0)

    @pl.when(head == 0)
    def _():
        bwin_ref[...] = jnp.zeros_like(bwin_ref)
        rope_ref[...] = jnp.zeros_like(rope_ref)

    back_heads = bh_ref[...]
    ge_ref[:, QN:] = matmul_tn(ol_ref[0], back_heads).astype(bf16)
    back_olatent = matmul_nt(back_heads, w_ref[:, QN:]).astype(bf16)
    scores = matmul_nt(qf_ref[0], win_ref[...])
    probs = jnp.exp(scores * scale + bias_ref[...] - lse_ref[0][:, :1])
    back_probs = matmul_nt(back_olatent, win_ref[:, :LATENT])
    delta = jnp.sum(probs * back_probs, axis=1, keepdims=True)
    back_scores = (probs * (back_probs - delta) * scale).astype(bf16)
    bwin_ref[...] += matmul_tn(back_scores, qf_ref[0])
    bwin_ref[:, :LATENT] += matmul_tn(probs.astype(bf16), back_olatent)
    back_q = matmul(back_scores, win_ref[...])
    back_qlatent = back_q[:, :LATENT].astype(bf16)
    ge_ref[:, :QN] = matmul_tn(back_qlatent, qn_ref[...]).astype(bf16)
    bqn_ref[...] = matmul(back_qlatent, w_ref[:, :QN]).astype(bf16)
    halves = back_q[:, LATENT:]
    lane = lax.broadcasted_iota(jnp.int32, halves.shape, 1)
    crossed = jnp.where(lane < 32, pltpu.roll(halves, 96, 1), pltpu.roll(halves, 32, 1))
    turned = (halves * cos_ref[...] + crossed * sin_ref[...]).astype(bf16)
    rope_ref[...] += matmul_nt(turned, rope_places(head)).astype(bf16)

    @pl.when(head == pl.num_programs(0) - 1)
    def _():
        own_ref[...] = bwin_ref[: own_ref.shape[0]]
        sib_ref[...] = bwin_ref[own_ref.shape[0] :].astype(bf16)


def to_chip_order(values, core):
    lane = lax.broadcasted_iota(jnp.int32, (values.shape[0], 128), 1)
    low = (lane & 32) == 0
    sides = ([], [])
    for at in range(0, 1024, 128):
        first, second = values[:, at : at + 128], values[:, 1024 + at : 1152 + at]
        sides[0].append(jnp.where(low, first, pltpu.roll(second, 32, 1)))
        sides[1].append(jnp.where(low, pltpu.roll(first, 96, 1), second))
    side0, side1 = (jnp.concatenate(side, axis=1) for side in sides)
    mine = core == 0
    return jnp.where(mine, side0, side1), jnp.where(mine, side1, side0)


def from_chip_order(own, sibling, core):
    lane = lax.broadcasted_iota(jnp.int32, (own.shape[0], 128), 1)
    low = (lane & 32) == 0
    mine = core == 0
    side0, side1 = jnp.where(mine, own, sibling), jnp.where(mine, sibling, own)
    rows = ([], [])
    for at in range(0, 1024, 128):
        first, second = side0[:, at : at + 128], side1[:, at : at + 128]
        rows[0].append(jnp.where(low, first, pltpu.roll(second, 32, 1)))
        rows[1].append(jnp.where(low, pltpu.roll(first, 96, 1), second))
    return jnp.concatenate(rows[0] + rows[1], axis=1)


def enter_kernel(core_ref, x_ref, g_ref, x_out, inverse_out, g_out):
    values = x_ref[...].astype(f32)
    mean = jnp.mean(values * values, axis=1, keepdims=True)
    inverse_out[...] = jnp.broadcast_to(lax.rsqrt(mean + epsilon), inverse_out.shape)
    own, sibling = to_chip_order(values, core_ref[0])
    x_out[:, :1024] = own
    x_out[:, 1024:] = sibling
    own, sibling = to_chip_order(g_ref[...].astype(f32), core_ref[0])
    g_out[:, :1024] = own.astype(bf16)
    g_out[:, 1024:] = sibling.astype(bf16)


def dispatch_kernel(core_ref, mid_ref, gain_ref, pick_ref, h_ref, inverse_ref, rows_ref, true_ref):
    @pl.when(pl.program_id(0) == 0)
    def _():
        mid = mid_ref[...]
        inverse = lax.rsqrt(jnp.mean(mid * mid, axis=1, keepdims=True) + epsilon)
        inverse_ref[...] = jnp.broadcast_to(inverse, inverse_ref.shape)
        low = (mid * inverse * gain_ref[...]).astype(bf16)
        h_ref[...] = low
        wide = low.astype(f32)
        true_ref[...] = from_chip_order(wide[:, :1024], wide[:, 1024:], core_ref[0]).astype(bf16)

    rows_ref[...] = matmul(pick_ref[...], true_ref[...]).astype(bf16)


def combine_kernel(core_ref, pick_ref, rows_ref, base_ref, out_ref, total_ref):
    step = pl.program_id(0)

    @pl.when(step == 0)
    def _():
        total_ref[...] = jnp.zeros_like(total_ref)

    total_ref[...] += matmul_tn(pick_ref[...], rows_ref[...])

    @pl.when(step == pl.num_programs(0) - 1)
    def _():
        own, sibling = to_chip_order(total_ref[...], core_ref[0])
        out_ref[:, :1024] = (own + base_ref[:, :1024]).astype(bf16)
        out_ref[:, 1024:] = (sibling + base_ref[:, 1024:]).astype(bf16)


def routed_kernel(core_ref, weight_ref, rows_ref, base_ref, out_ref, total_ref):
    step = pl.program_id(0)

    @pl.when(step == 0)
    def _():
        total_ref[...] = from_chip_order(base_ref[:, :1024], base_ref[:, 1024:], core_ref[0])

    high, low = split_low(weight_ref[...])
    total_ref[...] += matmul_tn(high, rows_ref[...]) + matmul_tn(low, rows_ref[...])

    @pl.when(step == pl.num_programs(0) - 1)
    def _():
        out_ref[...] = total_ref[...].astype(bf16)


def expert_kernel(
    second_ref, rows_ref, half_ref, first_ref, then_ref, gate_ref, up_ref, down_ref,
    grads_ref, hidden_ref, back_gate_ref, back_up_ref, row_ref,
):
    rows = rows_ref[...]
    second = second_ref[0] == 1
    half = half_ref[...]
    other = jnp.where(pl.program_id(0) == 0, first_ref[...], then_ref[...])
    low = jnp.where(second, other, half)
    high = jnp.where(second, half, other)
    grads_ref[:, :1024] = low
    grads_ref[:, 1024:] = high
    gate_pre = matmul_nt(rows, gate_ref[...])
    up_pre = matmul_nt(rows, up_ref[...])
    back_hidden = matmul_nt(low, down_ref[:, :1024]) + matmul_nt(high, down_ref[:, 1024:])
    sig = jax.nn.sigmoid(gate_pre)
    active = gate_pre * sig
    hidden_ref[...] = (active * up_pre).astype(bf16)
    back_gate = (back_hidden * up_pre * sig * (1.0 + gate_pre * (1.0 - sig))).astype(bf16)
    back_up = (back_hidden * active).astype(bf16)
    back_gate_ref[...] = back_gate
    back_up_ref[...] = back_up
    row_ref[...] = (matmul(back_gate, gate_ref[...]) + matmul(back_up, up_ref[...])).astype(bf16)


def shared_acts_kernel(all_ref, got_ref, acts_ref):
    width = acts_ref.shape[1] // 3
    gate, up, back = (
        all_ref[:, i * width : (i + 1) * width] + got_ref[:, i * width : (i + 1) * width].astype(f32)
        for i in range(3)
    )
    sig = jax.nn.sigmoid(gate)
    active = gate * sig
    acts_ref[:, :width] = (back * up * sig * (1.0 + gate * (1.0 - sig))).astype(bf16)
    acts_ref[:, width : 2 * width] = (back * active).astype(bf16)
    acts_ref[:, 2 * width :] = (active * up).astype(bf16)


def shared_rows_kernel(h_own_ref, h_sib_ref, g_ref, own_ref, sib_ref, out_ref):
    acts = jnp.concatenate([own_ref[...], sib_ref[...]], axis=0)
    last = pl.program_id(0) == pl.num_programs(0) - 1

    @pl.when(last)
    def _():
        out_ref[...] = matmul_tn(g_ref[...], acts).astype(bf16)

    @pl.when(jnp.logical_not(last))
    def _():
        h_two = jnp.concatenate([h_own_ref[...], h_sib_ref[...]], axis=0)
        out_ref[...] = matmul_tn(h_two, acts).astype(bf16)


def shared_wide_kernel(own_ref, sib_ref, w_ref, back_ref, part_ref, theirs_ref, total_ref):
    step = pl.program_id(0)
    tok = own_ref.shape[0]
    acts = jnp.concatenate([own_ref[...], sib_ref[...]], axis=0)
    wide = matmul_nt(acts, w_ref[...])

    @pl.when(step == 0)
    def _():
        total_ref[...] = wide

    @pl.when(step == 1)
    def _():
        total = total_ref[...] + wide
        back_ref[...] = total[:tok]
        theirs_ref[:, :1024] = total[tok:].astype(bf16)

    @pl.when(step == 2)
    def _():
        part_ref[...] = wide[:tok]
        theirs_ref[:, 1024:] = wide[tok:].astype(bf16)


def leave_kernel(core_ref, mid_ref, part_ref, other_ref, out_ref):
    true = from_chip_order(mid_ref[:, :1024], mid_ref[:, 1024:], core_ref[0])
    out_ref[...] = (true + (part_ref[...].astype(f32) + other_ref[...].astype(f32))).astype(bf16)


def grad_kernel(core_ref, grad_ref, out_ref):
    out_ref[...] = from_chip_order(grad_ref[:, :1024], grad_ref[:, 1024:], core_ref[0])


def scalar_spec():
    return pl.BlockSpec(memory_space=pltpu.SMEM)


def local_kernel(body, name, grid, in_specs, out_specs, out_shape, scratch=(), flops=0, moved=4 << 20):
    return pl.pallas_call(
        body,
        grid=(grid,),
        in_specs=in_specs,
        out_specs=out_specs,
        out_shape=out_shape,
        scratch_shapes=scratch,
        compiler_params=pltpu.CompilerParams(vmem_limit_bytes=VMEM_BYTES),
        cost_estimate=pl.CostEstimate(flops=flops, bytes_accessed=moved, transcendentals=0),
        name=name,
    )


def whole(shape):
    return pl.BlockSpec(shape, lambda h: (0,) * len(shape))


def attend(scale, q_nope, rope, w_expand, window, bias):
    tok, heads, keys = q_nope.shape[0], q_nope.shape[1] // QN, window.shape[0]
    return pl.pallas_call(
        functools.partial(attend_kernel, scale),
        grid=(heads,),
        in_specs=[
            pl.BlockSpec((tok, QN), lambda h: (0, h)),
            whole((tok, 512)),
            pl.BlockSpec((LATENT, QN + DV), lambda h: (0, h)),
            whole((keys, WIDE)),
            whole((tok, keys)),
        ],
        out_specs=[
            pl.BlockSpec((1, tok, WIDE), lambda h: (h, 0, 0)),
            pl.BlockSpec((1, tok, LATENT), lambda h: (h, 0, 0)),
            pl.BlockSpec((tok, DV), lambda h: (0, h)),
            pl.BlockSpec((1, tok, 128), lambda h: (h, 0, 0)),
        ],
        out_shape=[
            jax.ShapeDtypeStruct((heads, tok, WIDE), bf16),
            jax.ShapeDtypeStruct((heads, tok, LATENT), bf16),
            jax.ShapeDtypeStruct((tok, heads * DV), bf16),
            jax.ShapeDtypeStruct((heads, tok, 128), f32),
        ],
        compiler_params=pltpu.CompilerParams(vmem_limit_bytes=VMEM_BYTES),
        cost_estimate=pl.CostEstimate(
            flops=heads * tok * keys * 2400, bytes_accessed=12 << 20, transcendentals=heads * tok * keys
        ),
        name="attend",
    )(q_nope, rope, w_expand, window, bias)


def attend_back(scale, back_heads, w_expand, window, bias, q_full, q_nope, o_latent, log_total, cos, sin):
    tok, heads, keys = q_nope.shape[0], q_nope.shape[1] // QN, window.shape[0]
    return pl.pallas_call(
        functools.partial(attend_back_kernel, scale),
        grid=(heads,),
        in_specs=[
            pl.BlockSpec((tok, DV), lambda h: (0, h)),
            pl.BlockSpec((LATENT, QN + DV), lambda h: (0, h)),
            whole((keys, WIDE)),
            whole((tok, keys)),
            pl.BlockSpec((1, tok, WIDE), lambda h: (h, 0, 0)),
            pl.BlockSpec((tok, QN), lambda h: (0, h)),
            pl.BlockSpec((1, tok, LATENT), lambda h: (h, 0, 0)),
            pl.BlockSpec((1, tok, 128), lambda h: (h, 0, 0)),
            whole((tok, 128)),
            whole((tok, 128)),
        ],
        out_specs=[
            pl.BlockSpec((LATENT, QN + DV), lambda h: (0, h)),
            pl.BlockSpec((tok, QN), lambda h: (0, h)),
            whole((tok, 512)),
            whole((5 * tok, WIDE)),
            whole((4 * tok, WIDE)),
        ],
        out_shape=[
            jax.ShapeDtypeStruct((LATENT, heads * (QN + DV)), bf16),
            jax.ShapeDtypeStruct((tok, heads * QN), bf16),
            jax.ShapeDtypeStruct((tok, 512), bf16),
            jax.ShapeDtypeStruct((5 * tok, WIDE), f32),
            jax.ShapeDtypeStruct((4 * tok, WIDE), bf16),
        ],
        scratch_shapes=[pltpu.VMEM((keys, WIDE), f32)],
        compiler_params=pltpu.CompilerParams(vmem_limit_bytes=VMEM_BYTES),
        cost_estimate=pl.CostEstimate(
            flops=heads * tok * keys * 6400, bytes_accessed=20 << 20, transcendentals=heads * tok * keys
        ),
        name="attend_back",
    )(back_heads, w_expand, window, bias, q_full, q_nope, o_latent, log_total, cos, sin)


def shards(
    hidden_in,
    prenorm,
    query_proj,
    latent_proj,
    midnorm,
    expand_proj,
    output_proj,
    postnorm,
    shared_gate,
    shared_up,
    shared_down,
    expert_gate,
    expert_up,
    expert_down,
    segments,
    routes,
    route_weights,
    cotangent,
):
    dp = lax.axis_index("dp")
    core = lax.axis_index("core")
    chip = lax.axis_index("y") * 4 + lax.axis_index("z")
    tok = hidden_in.shape[0]
    heads = query_proj.shape[1] // (QN + QR)
    half = D // 2
    expert_pos = chip * 2 + core
    score_scale = 1.0 / math.sqrt(QN + QR)

    y_pos = lax.axis_index("y")
    z_pos = lax.axis_index("z")
    y_low = y_pos < 2
    y_outer = (y_pos == 0) | (y_pos == 3)
    fs = shared_gate.shape[1]

    gains = jnp.stack([prenorm, postnorm, jnp.pad(midnorm, (0, 24))], axis=1)
    q_cols = query_proj.reshape(32, heads, QN + QR)
    l_cols = latent_proj[:, :LATENT].reshape(32, 2, 16, 2, 8).transpose(0, 3, 2, 1, 4)
    pack = jnp.concatenate(
        [
            q_cols[:, :, :QN].reshape(32, heads * QN),
            q_cols[:, :, QN : QN + 32].reshape(32, heads * 32),
            q_cols[:, :, QN + 32 :].reshape(32, heads * 32),
            l_cols.reshape(32, LATENT),
            latent_proj[:, LATENT:],
            jnp.pad(gains, ((0, 0), (0, 61))),
            output_proj.T,
            expand_proj.reshape(32, 512),
        ],
        axis=1,
    )
    pair, shared_gate, shared_up, shared_down, y_late, z_late, segments = together(
        gather_dp(pack, dp), shared_gate, shared_up, shared_down, y_pos, z_pos, segments
    )
    pack_c = jnp.concatenate([shared_gate, shared_up, shared_down.T], axis=1)

    place = jnp.arange(D, dtype=jnp.int32)
    place_l = jnp.arange(LATENT, dtype=jnp.int32)
    mid_at = ((place // 1024) ^ core) * 256 + (place // 32 % 32) * 8 + place % 32
    perm_m = ((mid_at[:, None] == place_l[None, :]) & (place % 32 < 8)[:, None]).astype(bf16)
    core_at = core.reshape(1)

    def near_low(values):
        low, high = values[:, :512], values[:, 512:]
        return jnp.where(y_low, low, high), jnp.where(y_low, high, low)

    def near_outer(values):
        ends = jnp.concatenate([values[:, :256], values[:, 768:]], axis=1)
        middle = values[:, 256:768]
        return jnp.where(y_outer, ends, middle), jnp.where(y_outer, middle, ends)

    def join_low(own, other):
        return jnp.concatenate(
            [jnp.where(y_low, own, other), jnp.where(y_low, other, own)], axis=1
        )

    def join_outer(own, other):
        ends = jnp.where(y_outer, own, other)
        middle = jnp.where(y_outer, other, own)
        return jnp.concatenate([ends[:, :256], middle, ends[:, 256:]], axis=1)

    cuts = (0, 1024, 2176, 3200)
    chip_rows = [pair[:, a:b].reshape(1, 1, 64, b - a) for a, b in zip(cuts, cuts[1:])]
    chip_rows.append(pair[:, 3200:].reshape(1, 1, 16, 2048))
    along_z, along_y = ("z", z_pos, 1), ("y", y_pos, 0)
    firsts = [along_z + (False,), along_z + (True,), along_y + (False,), along_y + (True,)]
    seconds = [along_y + (False,), along_y + (True,), along_z + (False,), along_z + (True,)]

    def pairs(blocks, got, axes):
        return [
            merged(own, other, pos >= 2 if cross else pos % 2 == 1, dim)
            for own, other, (_, pos, dim, cross) in zip(blocks, got, axes)
        ]

    pair_c = gather_dp(pack_c, dp)
    blocks, got, pair_c, core_at, hidden_in, cotangent, routes, segments, y_late, z_late = together(
        chip_rows, gather_step(chip_rows, firsts, False), pair_c, core_at, hidden_in, cotangent,
        routes, segments, y_late, z_late,
    )
    blocks = pairs(blocks, got, firsts)
    blocks, got = together(blocks, gather_step(blocks, firsts, True))
    blocks = [joined(o, g, p, c, d) for o, g, (_, p, d, c) in zip(blocks, got, firsts)]
    blocks, got = together(blocks, gather_step(blocks, seconds, False))
    blocks = pairs(blocks, got, seconds)
    got = gather_step(blocks, seconds, True)
    near_sib = [swapped(block, "core") for block in blocks[:2]]

    inputs, inverse_one, up_low = local_kernel(
        enter_kernel,
        "enter",
        1,
        [scalar_spec(), whole((tok, D)), whole((tok, D))],
        [whole((tok, D)), whole((tok, 128)), whole((tok, D))],
        [
            jax.ShapeDtypeStruct((tok, D), f32),
            jax.ShapeDtypeStruct((tok, 128), f32),
            jax.ShapeDtypeStruct((tok, D), bf16),
        ],
    )(core_at, hidden_in, cotangent)
    inverse_one = inverse_one[:, :1]

    expert_ids = jnp.arange(32, dtype=jnp.int32)
    hits = routes[:, :, None] == expert_ids[None, None, :]
    named = jnp.sum(hits.astype(f32), axis=1)
    weight_te = jnp.sum(jnp.where(hits, route_weights[:, :, None], 0.0), axis=1)
    order = jnp.arange(tok, dtype=jnp.int32)
    earlier = (order[:, None] > order[None, :]).astype(bf16)
    rank = matmul(earlier, named.astype(bf16))
    rank_et = jnp.where(named > 0.5, rank, -1.0).T
    slot_ids = jnp.arange(SLOTS, dtype=jnp.int32).astype(f32)
    taken = rank_et[:, None, :] == slot_ids[None, :, None]
    slot_pick = taken.astype(bf16).reshape(32 * SLOTS, tok)
    slot_weight = jnp.where(taken, weight_te.T[:, None, :], 0.0).reshape(32 * SLOTS, tok)
    slot_pick, slot_weight = together(slot_pick, slot_weight)
    weight_hi, weight_lo = split_low(slot_weight)

    def exchange(rows):
        blocks = rows.reshape(32, SLOTS, rows.shape[1])
        return lax.all_to_all(blocks, EXPERT, split_axis=0, concat_axis=0, tiled=True).reshape(
            rows.shape
        )

    second = lax.axis_index("tensor") == 1
    grad_cols = jnp.where(second, cotangent[:, half:], cotangent[:, :half])
    grad_send = (matmul(weight_hi, grad_cols) + matmul(weight_lo, grad_cols)).astype(bf16)
    block_chip = jnp.concatenate(
        [chip - 4 + jnp.arange(5, dtype=jnp.int32), chip - 4 + core + jnp.arange(4, dtype=jnp.int32)]
    )
    block_core = jnp.concatenate(
        [jnp.full((5,), core, jnp.int32), jnp.full((4,), 1 - core, jnp.int32)]
    )
    block_id = block_chip * 2 + block_core
    seg_blocks = lax.dynamic_slice_in_dim(segments.reshape(2, 32, tok), dp, 1, 0)[0]
    chosen = jnp.arange(32, dtype=jnp.int32)[None, :, None] == block_id[:, None, None]
    seg_keys = jnp.sum(jnp.where(chosen, seg_blocks[None] + 1, 0), axis=1).reshape(9 * tok) - 1
    seg_query = lax.dynamic_index_in_dim(seg_blocks, expert_pos, 0, keepdims=False)
    key_pos = (block_id[:, None] * tok + jnp.arange(tok, dtype=jnp.int32)[None, :]).reshape(9 * tok)
    query_pos = expert_pos * tok + jnp.arange(tok, dtype=jnp.int32)
    offsets = query_pos[:, None] - key_pos[None, :]
    visible = (seg_query[:, None] == seg_keys[None, :]) & (offsets >= 0) & (offsets < WIN)

    bias = jnp.where(visible, 0.0, neg_big)
    positions = (expert_pos * tok + jnp.arange(tok, dtype=jnp.int32)).astype(f32)
    cosine, sine_tab = rope_tables(positions, QR)
    cos_all = jnp.tile(cosine, (1, heads))
    sin_all = jnp.tile(sine_tab, (1, heads))

    (
        blocks, got, inputs, inverse_one, up_low, slot_pick, slot_weight, grad_send, pair_c, bias,
        cosine, sine_tab, cos_all, sin_all, perm_m,
    ) = together(
        blocks, got, inputs, inverse_one, up_low, slot_pick, slot_weight, grad_send, pair_c, bias,
        cosine, sine_tab, cos_all, sin_all, perm_m,
    )
    grad_half = exchange(grad_send)
    upstream = up_low.astype(f32)
    q_parts = [
        w.reshape(512, 1024) for w in (blocks[0], got[0], near_sib[0], swapped(got[0], "core"))
    ]
    l_parts = [
        w.reshape(512, 1152) for w in (blocks[1], got[1], near_sib[1], swapped(got[1], "core"))
    ]
    own_c = lax.all_gather(pair_c, PLANE, axis=0, tiled=True)
    up_pair = both_cores(up_low[:, :half], swapped(up_low[:, half:], "core"))

    pick = jnp.eye(8, 64, dtype=bf16)
    gain_parts = [matmul_nt(pick, w[:, 1088:]) for w in l_parts]
    gain_rows = jnp.concatenate(
        [join_outer(gain_parts[0], gain_parts[1]), join_outer(gain_parts[2], gain_parts[3])], axis=1
    )
    gain_one = gain_rows[0]
    gain_two = gain_rows[1]
    gain_mid = matmul(gain_rows.astype(bf16), perm_m)[2]

    h_one = (inputs * inverse_one * gain_one).astype(bf16)
    h_parts = near_outer(h_one[:, :half]) + near_outer(h_one[:, half:])
    kv_all = sum(matmul(h, w) for h, w in zip(h_parts, l_parts))
    h_parts = near_low(h_one[:, :half]) + near_low(h_one[:, half:])
    q_nope = sum(matmul(h, w) for h, w in zip(h_parts, q_parts)).astype(bf16)
    q_first = kv_all[:, :256]
    q_second = kv_all[:, 256:512]
    kv_pre = kv_all[:, 512:1088]
    latent_raw = kv_pre[:, :LATENT]
    latent_normed, inverse_mid = rms_forward(latent_raw, gain_mid)
    latent = jnp.concatenate(
        [
            latent_normed,
            rotate(kv_pre[:, LATENT:], cosine, sine_tab),
            jnp.zeros((tok, WIDE - LATENT - QR), f32),
        ],
        axis=1,
    ).astype(bf16)
    latent, blocks, got = together(latent, blocks[2:], got[2:])
    w_out_own = joined(blocks[0], got[0], z_pos, False, 1).reshape(half, heads * DV)
    w_out_sib = swapped(w_out_own, "core")
    x_own = joined(blocks[1], got[1], z_pos, True, 1).reshape(256, heads * (QN + DV))
    x_sib = swapped(x_own, "core")
    w_expand = jnp.concatenate(
        [jnp.where(core == 0, x_own, x_sib), jnp.where(core == 0, x_sib, x_own)], axis=0
    )
    rope = jnp.concatenate(
        [q_first * cos_all - q_second * sin_all, q_first * sin_all + q_second * cos_all], axis=1
    ).astype(bf16)
    latent_other = swapped(latent, "core")
    both = jnp.stack(
        [jnp.where(core == 0, latent, latent_other), jnp.where(core == 0, latent_other, latent)]
    )
    nearer, farther, both, q_nope, rope, w_expand = together(
        core_shift(both, 1, 3), core_shift(both, 2, 4), both, q_nope, rope, w_expand
    )
    held = jnp.stack([farther, nearer])
    held_other = swapped(held, "core")
    chips = jnp.concatenate(
        [
            jnp.where(core == 0, held_other, held),
            jnp.where(core == 0, held, held_other),
            both[None],
        ],
        axis=0,
    )
    own_blocks = lax.dynamic_index_in_dim(chips, core, 1, keepdims=False)
    sib_blocks = lax.dynamic_slice_in_dim(
        lax.dynamic_index_in_dim(chips, 1 - core, 1, keepdims=False), core, 4, 0
    )
    window = jnp.concatenate([own_blocks, sib_blocks], axis=0).reshape(9 * tok, WIDE)
    window, grad_half = together(window, grad_half)
    q_full, o_latent, o_heads, log_total = attend(
        score_scale, q_nope, rope, w_expand, window, bias
    )
    o_part = jnp.concatenate(
        [matmul_nt(o_heads, w_out_own), matmul_nt(o_heads, w_out_sib)], axis=1
    ).astype(bf16)
    o_part, grad_first = together(o_part, swapped(grad_half[:512], "tensor"))
    mid = inputs + (o_part.astype(f32) + swapped(o_part, "tensor").astype(f32))
    h_one_pair = both_cores(h_one[:, :half], swapped(h_one[:, half:], "core"))
    mid, grad_half, h_one_pair = together(mid, grad_half, h_one_pair)
    grad_then = swapped(grad_half[512:], "tensor")

    slots = 32 * SLOTS
    h_two, inverse_two, send_rows = local_kernel(
        dispatch_kernel,
        "dispatch",
        4,
        [
            scalar_spec(),
            whole((tok, D)),
            whole((1, D)),
            pl.BlockSpec((slots // 4, tok), lambda i: (i, 0)),
        ],
        [
            whole((tok, D)),
            whole((tok, 128)),
            pl.BlockSpec((slots // 4, D), lambda i: (i, 0)),
        ],
        [
            jax.ShapeDtypeStruct((tok, D), bf16),
            jax.ShapeDtypeStruct((tok, 128), f32),
            jax.ShapeDtypeStruct((slots, D), bf16),
        ],
        [pltpu.VMEM((tok, D), bf16)],
        flops=2 * slots * tok * D,
        moved=6 << 20,
    )(core_at, mid, gain_two[None, :], slot_pick)
    inverse_two = inverse_two[:, :1]
    expert_rows = exchange(send_rows)

    h_two_other = swapped(h_two[:, half:], "core")
    h_two_pair = both_cores(h_two[:, :half], h_two_other)
    s_all = jnp.concatenate(
        [matmul(h_two_pair, own_c[:, : 2 * fs]), matmul(up_pair, own_c[:, 2 * fs :])], axis=1
    )
    s_acts = local_kernel(
        shared_acts_kernel,
        "shared_acts",
        1,
        [whole((tok, 3 * fs)), whole((tok, 3 * fs))],
        whole((tok, 3 * fs)),
        jax.ShapeDtypeStruct((tok, 3 * fs), bf16),
    )(s_all, swapped(s_all[tok:].astype(bf16), "core"))
    s_other = swapped(s_acts, "core")

    def third(rows):
        return pl.BlockSpec((rows, fs), lambda i: (0, i))

    shared_rows = local_kernel(
        shared_rows_kernel,
        "shared_rows",
        3,
        [whole((tok, half)), whole((tok, half)), whole((2 * tok, half)), third(tok), third(tok)],
        third(half),
        jax.ShapeDtypeStruct((half, 3 * fs), bf16),
        flops=4 * tok * half * 3 * fs,
        moved=12 << 20,
    )(h_two[:, :half], h_two_other, up_pair, s_acts, s_other)
    expert_rows, s_acts, s_other, shared_rows, grad_then = together(
        expert_rows, s_acts, s_other, shared_rows, grad_then
    )
    shared_part = lax.psum_scatter(shared_rows, PLANE, scatter_dimension=0, tiled=True)
    hidden_units = expert_gate.shape[2]

    def rows_of(width):
        return pl.BlockSpec((slots // 2, width), lambda i: (i, 0))

    grad_rows, hidden, back_gate, back_up, row_grad = local_kernel(
        expert_kernel,
        "experts",
        2,
        [
            scalar_spec(),
            rows_of(D),
            rows_of(half),
            whole((slots // 2, half)),
            whole((slots // 2, half)),
            whole((hidden_units, D)),
            whole((hidden_units, D)),
            whole((hidden_units, D)),
        ],
        [rows_of(D), rows_of(hidden_units), rows_of(hidden_units), rows_of(hidden_units), rows_of(D)],
        [
            jax.ShapeDtypeStruct((slots, D), bf16),
            jax.ShapeDtypeStruct((slots, hidden_units), bf16),
            jax.ShapeDtypeStruct((slots, hidden_units), bf16),
            jax.ShapeDtypeStruct((slots, hidden_units), bf16),
            jax.ShapeDtypeStruct((slots, D), bf16),
        ],
        flops=10 * slots * D * hidden_units,
        moved=26 << 20,
    )(
        second.astype(jnp.int32).reshape(1),
        expert_rows,
        grad_half,
        grad_first,
        grad_then,
        expert_gate[0].T,
        expert_up[0].T,
        expert_down[0],
    )
    row_back = exchange(row_grad)
    down_low = [
        matmul_tn(hidden, grad_rows[:, :1536]).astype(bf16),
        matmul_tn(hidden, grad_rows[:, 1536:]).astype(bf16),
    ]
    down_got = swapped(down_low[0], "dp")
    down_low[0], s_acts, s_other, hidden, back_gate, back_up = together(
        down_low[0], s_acts, s_other, hidden, back_gate, back_up
    )
    back_mine, part_mine, wide_theirs = local_kernel(
        shared_wide_kernel,
        "shared_wide",
        3,
        [third(tok), third(tok), third(half)],
        [whole((tok, half)), whole((tok, half)), whole((tok, D))],
        [
            jax.ShapeDtypeStruct((tok, half), f32),
            jax.ShapeDtypeStruct((tok, half), f32),
            jax.ShapeDtypeStruct((tok, D), bf16),
        ],
        [pltpu.VMEM((2 * tok, half), f32)],
        flops=4 * tok * half * 3 * fs,
        moved=12 << 20,
    )(s_acts, s_other, own_c)
    wide_got = swapped(wide_theirs, "core").astype(f32)
    shared_back = jnp.concatenate([back_mine, wide_got[:, :half]], axis=1)
    s_part = jnp.concatenate([part_mine, wide_got[:, half:]], axis=1)

    e_part = matmul(hidden, expert_down[0]).astype(bf16)
    gate_low = [
        matmul_tn(expert_rows[:, a:b], back_gate).astype(bf16)
        for a, b in ((0, 512), (512, 1280), (1280, D))
    ]
    up_low_grad = [
        matmul_tn(expert_rows[:, a:b], back_up).astype(bf16) for a, b in ((0, half), (half, D))
    ]
    row_back, down_got, gate_low, up_low_grad, e_part, s_part, shared_back = together(
        row_back, down_got, gate_low, up_low_grad, e_part, s_part, shared_back
    )
    returned = exchange(e_part)
    back_part = local_kernel(
        combine_kernel,
        "combine",
        4,
        [
            scalar_spec(),
            pl.BlockSpec((slots // 4, tok), lambda i: (i, 0)),
            pl.BlockSpec((slots // 4, D), lambda i: (i, 0)),
            whole((tok, D)),
        ],
        whole((tok, D)),
        jax.ShapeDtypeStruct((tok, D), bf16),
        [pltpu.VMEM((tok, D), f32)],
        flops=2 * slots * tok * D,
        moved=6 << 20,
    )(core_at, slot_pick, row_back, shared_back)
    back_two = back_part.astype(f32) + swapped(back_part, "tensor").astype(f32)
    back_midnorm, grad_gain_two = rms_backward(mid, inverse_two, gain_two, back_two)
    back_mid = upstream + back_midnorm
    back_attn = back_mid.astype(bf16)
    back_attn, grad_gain_two, back_mid, gate_low, up_low_grad, down_low = together(
        back_attn, grad_gain_two, back_mid, gate_low, up_low_grad, down_low
    )
    down_got = [down_got, swapped(down_low[1], "dp")]
    gate_got = [swapped(part, "dp") for part in gate_low]
    up_got = [swapped(part, "dp") for part in up_low_grad]

    attn_pair = both_cores(back_attn[:, :half], swapped(back_attn[:, half:], "core"))
    heads_pair = both_cores(o_heads, swapped(o_heads, "core"))
    gain_low = grad_gain_two.astype(bf16)
    gain_sum = add_low(gain_low[:half], swapped(gain_low[half:], "core"))
    gain_col = jnp.broadcast_to(gain_sum[:, None], (half, 128))

    back_heads = (
        matmul(back_attn[:, :half], w_out_own) + matmul(back_attn[:, half:], w_out_sib)
    ).astype(bf16)
    pad_lanes = jnp.zeros((tok, 64), f32)
    grad_expand, back_qnope, back_rope, back_own, back_sib = attend_back(
        score_scale,
        back_heads,
        w_expand,
        window,
        bias,
        q_full,
        q_nope,
        o_latent,
        log_total,
        jnp.concatenate([cosine, cosine, pad_lanes], axis=1),
        jnp.concatenate([sine_tab, -sine_tab, pad_lanes], axis=1),
    )
    back_qnope, back_rope, back_own, back_sib, grad_expand, down_got[1], gate_got[0] = together(
        back_qnope, back_rope, back_own, back_sib, grad_expand, down_got[1], gate_got[0]
    )
    acts_q = jnp.concatenate([back_qnope, back_rope], axis=1)
    expand_mine = lax.dynamic_slice_in_dim(grad_expand, core * 256, 256, 0)
    expand_theirs = lax.dynamic_slice_in_dim(grad_expand, 256 - core * 256, 256, 0)
    from_sib, acts_other, expand_other, acts_q, expand_mine, heads_pair, attn_pair, down_low = together(
        swapped(back_sib, "core"),
        swapped(acts_q, "core"),
        swapped(expand_theirs, "core"),
        acts_q,
        expand_mine,
        heads_pair,
        attn_pair,
        down_low,
    )

    from_sib = from_sib.astype(f32).reshape(4, tok, WIDE)
    pad_block = jnp.zeros((1, tok, WIDE), f32)
    from_sib = jnp.where(
        core == 0,
        jnp.concatenate([pad_block, from_sib], axis=0),
        jnp.concatenate([from_sib, pad_block], axis=0),
    )
    chip_blocks = back_own.reshape(5, tok, WIDE) + from_sib
    shifts = [chip_shift(chip_blocks[4 - k].astype(bf16), -k) for k in (4, 3, 2, 1)]

    acts_q = both_cores(acts_q, acts_other)
    rows_x = add_low(expand_mine, expand_other)
    chip_last, shifts, acts_q, rows_x, shared_part, returned, gate_got[1] = together(
        chip_blocks[4], shifts, acts_q, rows_x, shared_part, returned, gate_got[1]
    )
    weight_rows = jnp.concatenate(
        [
            matmul_tn(h_one_pair, acts_q).astype(bf16),
            matmul_tn(attn_pair, heads_pair).astype(bf16),
            gain_col,
            rows_x.reshape(half, 512),
        ],
        axis=1,
    )
    weight_part = lax.psum_scatter(weight_rows, PLANE, scatter_dimension=0, tiled=True)

    back_latent = chip_last + sum(shift.astype(f32) for shift in shifts)

    back_raw, grad_gain_mid = rms_backward(
        latent_raw, inverse_mid, gain_mid, back_latent[:, :LATENT]
    )
    back_kvpre = jnp.concatenate(
        [back_raw, rotate(back_latent[:, LATENT : LATENT + QR], cosine, -sine_tab)], axis=1
    ).astype(bf16)
    kv_pair = both_cores(back_kvpre, swapped(back_kvpre, "core"))
    mid_low = grad_gain_mid.astype(bf16)
    mid_sum = (mid_low.astype(f32) + swapped(mid_low, "core").astype(f32)).astype(bf16)
    mid_col = matmul_nt(perm_m[:half], jnp.broadcast_to(mid_sum[None, :], (64, LATENT)))
    rows_l = jnp.concatenate([matmul_tn(h_one_pair, kv_pair), mid_col], axis=1).astype(bf16)
    (
        rows_l, gate_got[2], returned, back_mid, gate_low, up_low_grad, back_qnope, back_rope, down_low,
        shared_part,
    ) = together(
        rows_l, gate_got[2], returned, back_mid, gate_low, up_low_grad, back_qnope, back_rope, down_low,
        shared_part,
    )
    down_sum = summed(down_low, down_got, 1)
    l_blocks = lax.all_to_all(
        rows_l.reshape(16, 64, 640), PLANE, split_axis=0, concat_axis=0, tiled=True
    )
    out_low = local_kernel(
        routed_kernel,
        "routed",
        4,
        [
            scalar_spec(),
            pl.BlockSpec((slots // 4, tok), lambda i: (i, 0)),
            pl.BlockSpec((slots // 4, D), lambda i: (i, 0)),
            whole((tok, D)),
        ],
        whole((tok, D)),
        jax.ShapeDtypeStruct((tok, D), bf16),
        [pltpu.VMEM((tok, D), f32)],
        flops=4 * slots * tok * D,
        moved=6 << 20,
    )(core_at, slot_weight, returned, s_part)
    back_lane = jnp.concatenate([back_rope, back_kvpre, jnp.zeros((tok, 64), bf16)], axis=1)
    q_back = [matmul_nt(back_qnope, w) for w in q_parts]
    l_back = [matmul_nt(back_lane, w) for w in l_parts]
    one_part = jnp.concatenate(
        [
            join_low(q_back[0], q_back[1]) + join_outer(l_back[0], l_back[1]),
            join_low(q_back[2], q_back[3]) + join_outer(l_back[2], l_back[3]),
        ],
        axis=1,
    ).astype(bf16)

    one_other = swapped(one_part, "tensor")
    out_other = swapped(out_low, "tensor")
    l_blocks, up_got[0], one_part, out_low, down_sum, shared_part = together(
        l_blocks, up_got[0], one_part, out_low, down_sum, shared_part
    )
    shared_mine = mine_of(shared_part.reshape(2, 32, 3 * fs), dp)
    shared_other = swapped(theirs_of(shared_part.reshape(2, 32, 3 * fs), dp), "dp")
    gate_sum = summed(gate_low, gate_got, 0)
    l_part = jnp.sum(l_blocks.astype(f32), axis=0).astype(bf16)
    weight_part, l_part, up_got[1], gate_sum, shared_mine, shared_other = together(
        weight_part, l_part, up_got[1], gate_sum, shared_mine, shared_other
    )
    shared_grads = shared_mine.astype(f32) + shared_other.astype(f32)
    sums = finish_rows(jnp.concatenate([weight_part, l_part], axis=1), dp)
    l_sum = sums[:, 3200:]

    back_one = one_part.astype(f32) + one_other.astype(f32)
    back_innorm, _ = rms_backward(inputs, inverse_one, gain_one, back_one)
    input_grad = local_kernel(
        grad_kernel,
        "input_order",
        1,
        [scalar_spec(), whole((tok, D))],
        whole((tok, D)),
        jax.ShapeDtypeStruct((tok, D), f32),
    )(core_at, back_mid + back_innorm)

    output = local_kernel(
        leave_kernel,
        "leave",
        1,
        [scalar_spec()] + [whole((tok, D))] * 3,
        whole((tok, D)),
        jax.ShapeDtypeStruct((tok, D), bf16),
    )(core_at, mid, out_low, out_other)

    weight_dots = jnp.sum(sums[:, :1536] * pack[:, :1536].astype(f32), axis=1) + jnp.sum(
        l_sum[:, :576] * pack[:, 1536:2112].astype(f32), axis=1
    )
    small = jnp.concatenate(
        [
            l_sum,
            (weight_dots / prenorm.astype(f32))[:, None],
            0.5 * sums[:, 2560:2561],
            jnp.zeros((32, 126), f32),
        ],
        axis=1,
    )
    small = small + swapped(small, "tensor")
    query_grad = jnp.concatenate(
        [
            sums[:, :1024].reshape(32, heads, QN),
            sums[:, 1024:1280].reshape(32, heads, 32),
            sums[:, 1280:1536].reshape(32, heads, 32),
        ],
        axis=2,
    ).reshape(32, heads * (QN + QR))
    latent_cols = small[:, :LATENT].reshape(32, 2, 16, 2, 8).transpose(0, 3, 2, 1, 4)
    latent_grad = jnp.concatenate(
        [latent_cols.reshape(32, LATENT), small[:, LATENT : LATENT + QR]], axis=1
    )

    return (
        output,
        input_grad,
        small[:, 640],
        query_grad,
        latent_grad,
        small[:8, 576],
        sums[:, 2688:3200].reshape(8, 2048),
        sums[:, 1536:2560].T,
        small[:, 641],
        shared_grads[:, :fs],
        shared_grads[:, fs : 2 * fs],
        shared_grads[:, 2 * fs :].T,
        gate_sum[None],
        summed(up_low_grad, up_got, 0)[None],
        down_sum[None],
    )


def solution(mesh):
    fine = Mesh(
        mesh.devices.reshape(2, 4, 4, 2, 2), ("dp", "y", "z", "core", "tensor")
    )
    rows = ("dp", "y", "z", "core")
    placed = (
        P(rows, None),
        P(rows),
        P(rows, "tensor"),
        P(rows, None),
        P(rows),
        P(rows, "tensor"),
        P("tensor", rows),
        P(rows),
        P(rows, "tensor"),
        P(rows, "tensor"),
        P("tensor", rows),
        P(EXPERT, None, "tensor"),
        P(EXPERT, None, "tensor"),
        P(EXPERT, "tensor", None),
        P(),
        P(rows, None),
        P(rows, None),
        P(rows, None),
    )
    return jax.shard_map(
        shards,
        mesh=fine,
        in_specs=placed,
        out_specs=(
            P(rows, None),
            P(rows, None),
            P(rows),
            P(rows, "tensor"),
            P(rows, None),
            P(rows),
            P(rows, "tensor"),
            P("tensor", rows),
            P(rows),
            P(rows, "tensor"),
            P(rows, "tensor"),
            P("tensor", rows),
            P(EXPERT, None, "tensor"),
            P(EXPERT, None, "tensor"),
            P(EXPERT, "tensor", None),
        ),
        check_vma=False,
    )
```
